32 devices in a mesh: dp: 8 (over z, y), tensor: 4 (over x, core).
Axes of the slice: x: 2, y: 2, z: 4, core: 2. Of those that a mesh axis runs over, the one named last changes fastest.
Arguments:
- block_input: bfloat16 [2560, 2304], P(('dp', 'tensor')), may hold values from -6 to 6
- w_qkv: bfloat16 [3, 2304, 2304], P(None, 'dp', 'tensor'), may hold values from -0.1875 to 0.1875
- w_out: bfloat16 [2304, 2304], P('tensor', 'dp'), may hold values from -1 to 1
- w_gate_up: bfloat16 [2, 2304, 5760], P(None, 'dp', 'tensor'), may hold values from -0.125 to 0.125
- w_down: bfloat16 [5760, 2304], P('tensor', 'dp'), may hold values from -0.25 to 0.25
- norm_gains: bfloat16 [2, 2304], P(None, 'dp'), may hold values from 0.099609375 to 1.8984375
- cotangent: bfloat16 [2560, 2304], P(('dp', 'tensor')), may hold values from -6 to 6
- tok_seg: int32 [2560], P('dp'), may hold values from 0 to 12, as said below
- tok_pos: int32 [2560], P('dp'), may hold values from 0 to 1407, as said below
- seg_parent: int32 [13], replicated, may hold values from -1 to 4, as said below
Outputs:
- output: float32 [2560, 2304], P(('dp', 'tensor'))
- grad_input: float32 [2560, 2304], P(('dp', 'tensor'))
- grad_w_qkv: float32 [3, 2304, 2304], P(None, 'dp', 'tensor')
- grad_w_out: float32 [2304, 2304], P('tensor', 'dp')
- grad_w_gate_up: float32 [2, 2304, 5760], P(None, 'dp', 'tensor')
- grad_w_down: float32 [5760, 2304], P('tensor', 'dp')
- grad_gains: float32 [2, 2304], P(None, ('dp', 'tensor'))
The draws below stay inside these ranges and needn't reach their ends.
Inputs may be any that keep to these rules, and one draw needn't show every extreme that they name: Segments are numbered in token order, so tok_seg never falls: first the 1 trunks of 1024 tokens, then 4 * 1 branches, then 8 * 1 leaves; branches hold 64 to 192 tokens and leaves 128 - 128 // 2 to 192. Every segment is present. `tok_pos`: A trunk's tokens count from 0; a branch continues after its trunk's 1024, a leaf after its trunk and its branch. Some leaf of the longest length lies under a branch of the longest length, so the largest position is reached. `seg_parent`: A trunk's parent is -1, a branch's is a trunk, a leaf's is a branch; every trunk has four branches and every branch two leaves. The first token and the last token lie in one tree.
All inputs are finite; a program needn't handle non-finite values.
Results may differ from the reference program's by a relative error of at most 0.02.
Values may be sent and summed in bfloat16 or wider, within the bound.
No kernel may reach another device: no remote copies, remote signals or barrier semaphores. Data moves between devices by JAX's collectives and lax.ppermute only.
A program may use at most 256 MiB of HBM per device.

```python
import math
import jax
import jax.numpy as jnp
from jax import lax

D = 2304
H = 36
HD = 64
FF = 5760
TRUNK = 1024
BRANCH = 128
LEAF = 128
TREE = 2560
TOKENS = 2560


def forest(key):
    key = jax.random.fold_in(key, 7)
    key_list = jax.random.split(key, 5)
    tree_count = TOKENS // TREE
    trunk_tree = jax.random.permutation(key_list[0], tree_count).astype(jnp.int32)
    branch_ids = jax.random.permutation(key_list[1], 4 * tree_count).astype(jnp.int32)
    leaf_ids = jax.random.permutation(key_list[2], 8 * tree_count).astype(jnp.int32)
    target = trunk_tree[0] * 8
    places = jnp.arange(8 * tree_count, dtype=jnp.int32)
    where_now = jnp.sum(jnp.where(leaf_ids == target, places, 0)).astype(jnp.int32)
    final_leaf = leaf_ids[8 * tree_count - 1]
    leaf_ids = jnp.where(places == where_now, final_leaf, leaf_ids)
    leaf_ids = jnp.where(places == 8 * tree_count - 1, target, leaf_ids).astype(jnp.int32)
    branch_split = (BRANCH // 2 + jax.random.randint(key_list[3], (2 * tree_count,), 0, BRANCH + 1)).astype(jnp.int32)
    branch_split = jnp.where(jnp.arange(2 * tree_count, dtype=jnp.int32) == 0, BRANCH // 2 + BRANCH, branch_split).astype(jnp.int32)
    branch_len = jnp.stack([branch_split, 2 * BRANCH - branch_split], axis=1).reshape(-1).astype(jnp.int32)
    leaf_split = (LEAF // 2 + jax.random.randint(key_list[4], (4 * tree_count,), 0, LEAF + 1)).astype(jnp.int32)
    leaf_split = jnp.where(jnp.arange(4 * tree_count, dtype=jnp.int32) == 0, LEAF // 2 + LEAF, leaf_split).astype(jnp.int32)
    leaf_len = jnp.stack([leaf_split, 2 * LEAF - leaf_split], axis=1).reshape(-1).astype(jnp.int32)
    seg_len = jnp.concatenate([jnp.full((tree_count,), TRUNK, jnp.int32), branch_len[branch_ids], leaf_len[leaf_ids]]).astype(jnp.int32)
    trunk_of_tree = jnp.zeros((tree_count,), jnp.int32).at[trunk_tree].set(jnp.arange(tree_count, dtype=jnp.int32))
    branch_slot = jnp.zeros((4 * tree_count,), jnp.int32).at[branch_ids].set(jnp.arange(4 * tree_count, dtype=jnp.int32))
    branch_parent = trunk_of_tree[branch_ids // 4]
    leaf_parent = tree_count + branch_slot[leaf_ids // 2]
    parents = jnp.concatenate([jnp.full((tree_count,), -1, jnp.int32), branch_parent, leaf_parent]).astype(jnp.int32)
    seg_offset = jnp.concatenate([jnp.zeros((tree_count,), jnp.int32), jnp.full((4 * tree_count,), TRUNK, jnp.int32), TRUNK + branch_len[leaf_ids // 2]]).astype(jnp.int32)
    seg_start = (jnp.cumsum(seg_len) - seg_len).astype(jnp.int32)
    segments = jnp.repeat(jnp.arange(13 * tree_count, dtype=jnp.int32), seg_len, total_repeat_length=TOKENS).astype(jnp.int32)
    positions = (seg_offset[segments] + jnp.arange(TOKENS, dtype=jnp.int32) - seg_start[segments]).astype(jnp.int32)
    return (segments, positions, parents)


def draw_tok_seg(key, part):
    return forest(key)[0]


def draw_tok_pos(key, part):
    return forest(key)[1]


def draw_seg_parent(key, part):
    return forest(key)[2]


def levels(own_key, dims, pieces, smallest, largest):
    def one(axis_at, parts):
        steps = jax.random.uniform(jax.random.fold_in(jax.random.fold_in(own_key, 6), axis_at), (parts,), jnp.float32, smallest / len(pieces), largest / len(pieces))
        return jnp.repeat(jnp.exp(steps), dims[axis_at] // parts).reshape((-1,) + (1,) * (len(dims) - axis_at - 1))

    gain = one(*pieces[0])
    for cut in pieces[1:]:
        gain = gain * one(*cut)
    return gain


def centred(own_key, extent, width, limit, cuts=(), kind=jnp.bfloat16):
    result = jax.random.normal(own_key, extent, jnp.float32) * width
    if len(cuts) > 0:
        result = levels(own_key, extent, cuts, -0.22, 0.18) * result
    return jnp.clip(result, min=-limit, max=limit).astype(kind)


def setup_inputs(seed: int = 0) -> dict:
    streams_of = jax.random.split(jax.random.key(seed), 11)
    return {
        "block_input": centred(streams_of[0], (TOKENS, D), 1.0, 6.0, ((0, 32),)),
        "w_qkv": centred(streams_of[1], (3, D, D), (D // 2) ** -0.5, 0.1875, ((1, 8), (2, 4))),
        "w_out": centred(streams_of[2], (D, D), (D // 64) ** -0.5, 1.0, ((0, 4), (1, 8))),
        "w_gate_up": centred(streams_of[3], (2, D, FF), D ** -0.5, 0.125, ((1, 8), (2, 4))),
        "w_down": centred(streams_of[4], (FF, D), (FF // 12) ** -0.5, 0.25, ((0, 4), (1, 8))),
        "norm_gains": jnp.clip(1.0 + 0.18 * jax.random.normal(streams_of[5], (2, D), jnp.float32), 0.099609375, 1.8984375).astype(jnp.bfloat16),
        "cotangent": centred(streams_of[6], (TOKENS, D), 1.0, 6.0, ((0, 32),)),
        "tok_seg": draw_tok_seg(jax.random.fold_in(streams_of[10], 71), 0),
        "tok_pos": draw_tok_pos(jax.random.fold_in(streams_of[10], 71), 0),
        "seg_parent": draw_seg_parent(jax.random.fold_in(streams_of[10], 71), 0),
    }


norm_eps = 1e-05
depth_scale = 1.4 / math.sqrt(40.0)
rope_base = 10000.0
far_below = -1e+30
highest = lax.Precision.HIGHEST

@jax.custom_vjp
def low(v):
    return lax.optimization_barrier(v.astype(jnp.bfloat16)).astype(jnp.float32)

@jax.custom_vjp
def low_back(v):
    return v

def low_keep(v):
    return (low(v), None)

def low_pass(kept, grad):
    return (grad,)

def back_keep(v):
    return (v, None)

def back_low(kept, grad):
    return (low(grad),)
low.defvjp(low_keep, low_pass)
low_back.defvjp(back_keep, back_low)

def lineage(segments, parents):
    seg_table = jnp.arange(parents.shape[0], dtype=jnp.int32)
    matches = segments[:, None] == seg_table[None, :]
    parent_seg = lax.optimization_barrier(jnp.sum(jnp.where(matches, parents[None, :], 0), axis=1)).astype(jnp.int32)
    matches = parent_seg[:, None] == seg_table[None, :]
    grand_seg = lax.optimization_barrier(jnp.sum(jnp.where(matches, parents[None, :], 0), axis=1)).astype(jnp.int32)
    grand_seg = jnp.where(parent_seg >= 0, grand_seg, -1).astype(jnp.int32)
    return (parent_seg, grand_seg)

def rope_tables(positions, head_width):
    half_size = head_width // 2
    frequency = jnp.power(rope_base, -2.0 * jnp.arange(half_size, dtype=jnp.float32) / head_width)
    angles = positions.astype(jnp.float32)[:, None] * frequency[None, :]
    return (jnp.cos(angles), jnp.sin(angles))

def rotate(values, cosine, sine_table):
    half_size = values.shape[-1] // 2
    front = values[..., :half_size]
    latter = values[..., half_size:]
    cos_rows = cosine[:, None, :]
    sin_rows = sine_table[:, None, :]
    return jnp.concatenate([front * cos_rows - latter * sin_rows, latter * cos_rows + front * sin_rows], axis=-1)

def rms_norm(values, gain_row):
    inv_rms = lax.rsqrt(lax.optimization_barrier(jnp.mean(values * values, axis=-1, keepdims=True)) + norm_eps)
    return low(values * inv_rms * gain_row)

def one_tree(portion):
    tree_q, tree_k, tree_v, tree_seg, tree_parent, tree_grand, tree_index = portion
    block_rows = 512 if TREE % 512 == 0 else TREE
    block_count = TREE // block_rows
    scale_factor = HD ** (-0.5)
    blocks = (tree_q.reshape(block_count, block_rows, H, HD), tree_seg.reshape(block_count, block_rows), tree_parent.reshape(block_count, block_rows), tree_grand.reshape(block_count, block_rows), tree_index.reshape(block_count, block_rows))

    def one_block(element):
        block_q, block_seg, block_parent, block_grand, block_index = element
        same = (tree_seg[None, :] == block_seg[:, None]) & (tree_index[None, :] <= block_index[:, None])
        allowed = same | (tree_seg[None, :] == block_parent[:, None]) | (tree_seg[None, :] == block_grand[:, None])
        raw_scores = low_back(jnp.einsum('qhd,khd->hqk', block_q, tree_k, precision=highest))
        scores = jnp.where(allowed[None], raw_scores * scale_factor, far_below)
        row_peak = lax.optimization_barrier(jnp.max(scores, axis=-1, keepdims=True))
        expo = jnp.exp(scores - row_peak)
        weights = low(expo / lax.optimization_barrier(jnp.sum(expo, axis=-1, keepdims=True)))
        mixed = jnp.einsum('hqk,khd->qhd', weights, tree_v, precision=highest)
        return mixed.reshape(block_rows, H * HD)
    return lax.map(jax.checkpoint(one_block), blocks).reshape(TREE, H * HD)

def tree_attention(queries, keys_all, values, info):
    segments, parent_seg, grand_seg, order, back = info
    token_count = queries.shape[0]
    tree_count = token_count // TREE
    index = jnp.arange(token_count, dtype=jnp.int32)

    def by_tree(array):
        return jnp.take(array, order, axis=0).reshape((tree_count, TREE) + array.shape[1:])
    portions = tuple((by_tree(array) for array in (queries, keys_all, values, segments, parent_seg, grand_seg, index)))
    mixed = lax.map(jax.checkpoint(one_tree), portions).reshape(token_count, H * HD)
    return jnp.take(mixed, back, axis=0)

def reference(block_input, w_qkv, w_out, w_gate_up, w_down, norm_gains, cotangent, tok_seg, tok_pos, seg_parent):
    parent_seg, grand_seg = lineage(tok_seg, seg_parent)
    root = jnp.where(parent_seg < 0, tok_seg, jnp.where(grand_seg < 0, parent_seg, grand_seg)).astype(jnp.int32)
    order = jnp.argsort(root, stable=True).astype(jnp.int32)
    back = jnp.zeros_like(order).at[order].set(jnp.arange(order.shape[0], dtype=jnp.int32))
    cosine, sine_table = rope_tables(tok_pos, HD)
    info = (tok_seg, parent_seg, grand_seg, order, back)

    def forward(input_f, qkv_f, out_f, gate_up_f, down_f, gain_f):
        normed_a = rms_norm(input_f, gain_f[0])
        q_pre = low_back(jnp.dot(normed_a, qkv_f[0], precision=highest))
        k_pre = low_back(jnp.dot(normed_a, qkv_f[1], precision=highest))
        v_pre = low(low_back(jnp.dot(normed_a, qkv_f[2], precision=highest)))
        head_shape = (input_f.shape[0], H, HD)
        queries = low(rotate(q_pre.reshape(head_shape), cosine, sine_table))
        keys_all = low(rotate(k_pre.reshape(head_shape), cosine, sine_table))
        attended = tree_attention(queries, keys_all, v_pre.reshape(head_shape), info)
        attended = low(low_back(attended))
        mid = input_f + depth_scale * low_back(jnp.dot(attended, out_f, precision=highest))
        normed_f = rms_norm(mid, gain_f[1])
        gate_pre = low_back(jnp.dot(normed_f, gate_up_f[0], precision=highest))
        up_pre = low_back(jnp.dot(normed_f, gate_up_f[1], precision=highest))
        hidden = low(jax.nn.silu(gate_pre) * up_pre)
        return mid + depth_scale * low_back(jnp.dot(hidden, down_f, precision=highest))
    primals = (block_input.astype(jnp.float32), w_qkv.astype(jnp.float32), w_out.astype(jnp.float32), w_gate_up.astype(jnp.float32), w_down.astype(jnp.float32), norm_gains.astype(jnp.float32))
    output, pullback = jax.vjp(forward, *primals)
    grads = pullback(cotangent.astype(jnp.float32))
    return (output, grads[0], grads[1], grads[2], grads[3], grads[4], grads[5])
```

```python
import math

import jax
import jax.numpy as jnp
from jax import lax
from jax.experimental import pallas as pl
from jax.experimental.pallas import tpu as pltpu
from jax.sharding import Mesh, PartitionSpec as P

HD = 64

norm_eps = 1e-05
depth_scale = 1.4 / math.sqrt(40.0)
rope_base = 10000.0
far_below = -1e30
f32 = jnp.float32
bf16 = jnp.bfloat16

PLANE = ("pb", "tx", "tc")
CHIPS = ("pb", "tx")
ROW = "za"


def dot(a, b, dims=((1,), (0,))):
    return lax.dot_general(a, b, (dims, ((), ())), preferred_element_type=f32)


def send_row(array, distance):
    return lax.ppermute(array, ROW, [(i, i ^ distance) for i in range(lax.axis_size(ROW))])


def swap_core(array):
    return lax.ppermute(array, "tc", [(0, 1), (1, 0)])


def row_gather(rows):
    count = lax.axis_size(ROW)
    return jnp.concatenate([rows] + [send_row(rows, k) for k in range(1, count)], axis=0)


def row_scatter(partial):
    count = lax.axis_size(ROW)
    height = partial.shape[0] // count
    total = partial[:height]
    for k in range(1, count):
        total = total + send_row(partial[k * height : (k + 1) * height].astype(bf16), k).astype(f32)
    return total


def after(array, done):
    return lax.optimization_barrier((array, done))[0]


def plane_scatter(left, right):
    core = lax.axis_index("tc")
    chips = lax.axis_size("pb") * lax.axis_size("tx")
    blocks = left.reshape(left.shape[0], chips, 2, -1)

    def half(which):
        part = lax.dynamic_index_in_dim(blocks, which, 2, keepdims=False)
        return dot(part.reshape(left.shape[0], -1), right, ((0,), (0,)))

    other = swap_core(half(1 - core).astype(bf16))
    total = (half(core) + other.astype(f32)).astype(bf16)
    total = total.reshape(chips, -1, total.shape[1])
    total = lax.all_to_all(total, CHIPS, 0, 0, tiled=True)
    return jnp.sum(total.astype(f32), axis=0).astype(bf16)


def turn(array):
    pairs = []
    for z in range(4):
        for tx in range(2):
            for tc in range(2):
                pairs.append((z * 4 + tx * 2 + tc, (tc * 2 + tx) * 4 + (z % 2) * 2 + z // 2))
    return lax.ppermute(array, ("za", "tx", "tc"), pairs)


def lineage(segments, parents):
    seg_table = jnp.arange(parents.shape[0], dtype=jnp.int32)
    matches = segments[:, None] == seg_table[None, :]
    parent_seg = jnp.sum(jnp.where(matches, parents[None, :], 0), axis=1)
    matches = parent_seg[:, None] == seg_table[None, :]
    grand_seg = jnp.sum(jnp.where(matches, parents[None, :], 0), axis=1)
    grand_seg = jnp.where(parent_seg >= 0, grand_seg, -1)
    return (parent_seg, grand_seg)


def rope_tables(positions):
    half_size = HD // 2
    frequency = jnp.power(rope_base, -2.0 * jnp.arange(half_size, dtype=f32) / HD)
    angles = positions.astype(f32)[:, None] * frequency[None, :]
    return (jnp.cos(angles), jnp.sin(angles))


def rotate(flat, cosine, sine_table):
    values = flat.reshape(flat.shape[0], -1, HD)
    front = values[..., : HD // 2]
    latter = values[..., HD // 2 :]
    cos_rows = cosine[:, None, :]
    sin_rows = sine_table[:, None, :]
    return jnp.concatenate(
        [front * cos_rows - latter * sin_rows, latter * cos_rows + front * sin_rows], axis=-1
    ).reshape(flat.shape)


def norm_back(upstream, unit_rows, inv_rms):
    return inv_rms * (upstream - unit_rows * jnp.mean(upstream * unit_rows, axis=-1, keepdims=True))


def inverse_rms(rows):
    return lax.rsqrt(jnp.mean(rows * rows, axis=-1, keepdims=True) + norm_eps)


def heads_of(flat):
    return flat.reshape(flat.shape[0], -1, HD)


def side_by_side(left, right):
    count = (right if left is None else left).shape[0]
    parts = [None if t is None else heads_of(t) for t in (left, right)]
    blank = jnp.zeros_like(next(t for t in parts if t is not None))
    parts = [blank if t is None else t for t in parts]
    return jnp.concatenate(parts, axis=2).reshape(count, -1)


def fill_bias(query_ref, key_ref, bias_ref):
    @pl.when(pl.program_id(0) == 0)
    def _():
        seg, parent, grand, index = (query_ref[:, n : n + 1] for n in range(4))

        def fill(n, none):
            key_seg, key_index = key_ref[n, 0:1, :], key_ref[n, 1:2, :]
            allowed = (
                ((key_seg == seg) & (key_index <= index)) | (key_seg == parent) | (key_seg == grand)
            )
            bias_ref[n] = jnp.where(allowed, 0.0, far_below)
            return none

        lax.fori_loop(0, key_ref.shape[0], fill, 0)


def in_token_order(ref, row, chunks):
    height = ref.shape[0] // chunks
    return jnp.concatenate(
        [ref[pl.ds(pl.multiple_of((n ^ row) * height, 16), height), :] for n in range(chunks)], axis=0
    )


def keys_of(kv_ref, row, quarter, part, spans):
    count = kv_ref.shape[0] // spans
    block = kv_ref[pl.ds(part * count, count), quarter ^ row]
    return block.reshape(-1, 2 * HD)


def lower(top, change, skip):
    if skip == 0:
        return change(top)
    return jnp.concatenate([top[:skip], change(top[skip:])], axis=0)


def attend_kernel(row_ref, query_ref, key_ref, q_ref, kv_ref, out_ref, bias_ref):
    chunks, height = kv_ref.shape[1:3]
    spans = key_ref.shape[0] // chunks
    row = row_ref[0]
    fill_bias(query_ref, key_ref, bias_ref)
    q = in_token_order(q_ref, row, chunks)

    def span(part, carry):
        peak, total, mixed = carry
        keys = [keys_of(kv_ref, row, n, part, spans) for n in range(chunks)]
        scores = [
            dot(q[n * height :], keys[n], ((1,), (1,))) + bias_ref[n * spans + part, n * height :, :]
            for n in range(chunks)
        ]
        new_peak = peak
        for n in range(chunks):
            high = jnp.max(scores[n], axis=1, keepdims=True)
            new_peak = lower(new_peak, lambda p: jnp.maximum(p, high), n * height)
        factor = jnp.exp(peak - new_peak)
        total = total * factor
        mixed = mixed * factor
        for n in range(chunks):
            weights = jnp.exp(scores[n] - new_peak[n * height :])
            added = jnp.sum(weights, axis=1, keepdims=True)
            total = lower(total, lambda v: v + added, n * height)
            values = dot(weights.astype(bf16), keys[n])
            mixed = lower(mixed, lambda v: v + values, n * height)
        return new_peak, total, mixed

    start = (
        jnp.full((q.shape[0], 1), far_below, f32),
        jnp.zeros((q.shape[0], 1), f32),
        jnp.zeros((q.shape[0], 2 * HD), f32),
    )
    peak, total, mixed = span(0, start) if spans == 1 else lax.fori_loop(0, spans, span, start)
    lane = lax.broadcasted_iota(jnp.int32, mixed.shape, 1)
    result = jnp.where(lane < HD, peak + jnp.log(total), mixed / total)
    for n in range(chunks):
        out_ref[pl.ds(pl.multiple_of((n ^ row) * height, 16), height), :] = result[
            n * height : (n + 1) * height
        ]


def attend_back_kernel(
    row_ref, query_ref, key_ref, q_ref, kv_ref, out_ref, grad_ref, grad_q_ref, grad_kv_ref, bias_ref
):
    chunks, height = kv_ref.shape[1:3]
    spans = key_ref.shape[0] // chunks
    count = kv_ref.shape[0] // spans
    row = row_ref[0]
    fill_bias(query_ref, key_ref, bias_ref)
    q = in_token_order(q_ref, row, chunks)
    grad = in_token_order(grad_ref, row, chunks)
    saved = in_token_order(out_ref, row, chunks)
    log_total = saved[:, 0:1]
    delta = jnp.sum(grad.astype(f32) * saved, axis=1, keepdims=True)

    def span(part, grad_q):
        for n in range(chunks):
            skip = n * height
            keys = keys_of(kv_ref, row, n, part, spans)
            scores = dot(q[skip:], keys, ((1,), (1,))) + bias_ref[n * spans + part, skip:, :]
            probs = jnp.exp(scores - log_total[skip:])
            grad_probs = dot(grad[skip:], keys, ((1,), (1,)))
            grad_scores = (probs * (grad_probs - delta[skip:])).astype(bf16)
            added = dot(grad_scores, q[skip:], ((0,), (0,))) + dot(
                probs.astype(bf16), grad[skip:], ((0,), (0,))
            )
            grad_kv_ref[pl.ds(part * count, count), n ^ row] = added.astype(bf16).reshape(
                count, height, 2 * HD
            )
            more = dot(grad_scores, keys)
            grad_q = lower(grad_q, lambda v: v + more, skip)
        return grad_q

    start = jnp.zeros((q.shape[0], 2 * HD), f32)
    grad_q = span(0, start) if spans == 1 else lax.fori_loop(0, spans, span, start)
    for n in range(chunks):
        grad_q_ref[pl.ds(pl.multiple_of((n ^ row) * height, 16), height), :] = grad_q[
            n * height : (n + 1) * height
        ]


def attention_specs(queries, kv, query_info, key_info):
    heads = queries.shape[1] // (2 * HD)
    rows = pl.BlockSpec((queries.shape[0], 2 * HD), lambda h: (0, h))
    keys = pl.BlockSpec(kv.shape[:3] + (2 * HD,), lambda h: (0, 0, 0, h))
    fixed = [
        pl.BlockSpec(memory_space=pltpu.SMEM),
        pl.BlockSpec(query_info.shape, lambda h: (0, 0)),
        pl.BlockSpec(key_info.shape, lambda h: (0, 0, 0)),
    ]
    bias = pltpu.VMEM((key_info.shape[0], queries.shape[0], key_info.shape[2]), f32)
    params = pltpu.CompilerParams(vmem_limit_bytes=56 * 2**20)
    return heads, rows, keys, fixed, bias, params


def attend(row, query_info, key_info, queries, kv):
    heads, rows, keys, fixed, bias, params = attention_specs(queries, kv, query_info, key_info)
    return pl.pallas_call(
        attend_kernel,
        grid=(heads,),
        in_specs=fixed + [rows, keys],
        out_specs=rows,
        out_shape=jax.ShapeDtypeStruct(queries.shape, f32),
        scratch_shapes=[bias],
        compiler_params=params,
    )(row, query_info, key_info, queries, kv)


def attend_back(row, query_info, key_info, queries, kv, saved, grad):
    heads, rows, keys, fixed, bias, params = attention_specs(queries, kv, query_info, key_info)
    return pl.pallas_call(
        attend_back_kernel,
        grid=(heads,),
        in_specs=fixed + [rows, keys, rows, rows],
        out_specs=[rows, keys],
        out_shape=[
            jax.ShapeDtypeStruct(queries.shape, f32),
            jax.ShapeDtypeStruct(kv.shape, bf16),
        ],
        scratch_shapes=[bias],
        compiler_params=params,
    )(row, query_info, key_info, queries, kv, saved, grad)


def on_device(
    block_input,
    w_qkv,
    w_out,
    w_gate_up,
    w_down,
    norm_gains,
    cotangent,
    tok_seg,
    tok_pos,
    seg_parent,
):
    rows_n, b_n, x_n, c_n = (lax.axis_size(n) for n in ("za", "pb", "tx", "tc"))
    z, b, x, c = (lax.axis_index(n) for n in ("za", "pb", "tx", "tc"))
    shares = x_n * c_n
    plane = b_n * shares
    own, width = block_input.shape
    piece = width // plane

    def to_plane(array):
        blocks = array.reshape(-1, c_n, x_n, b_n, piece)
        return blocks.transpose(0, 3, 2, 1, 4).reshape(array.shape)

    def from_plane(array):
        blocks = array.reshape(-1, b_n, x_n, c_n, piece)
        return blocks.transpose(0, 3, 2, 1, 4).reshape(array.shape)

    def untangle(array, axis, index):
        count = array.shape[axis]
        for bit in range(count.bit_length() - 1):
            step = 1 << bit
            shape = array.shape[:axis] + (count // (2 * step), 2, step) + array.shape[axis + 1 :]
            flipped = jnp.flip(array.reshape(shape), axis + 1).reshape(array.shape)
            array = jnp.where((index >> bit) & 1 == 1, flipped, array)
        return array

    small = jnp.concatenate(
        [norm_gains.astype(f32).reshape(-1), tok_seg.astype(f32), tok_pos.astype(f32)]
    )
    small = jnp.stack([small] + [send_row(small, k) for k in range(1, rows_n)])
    across_b = [
        lax.ppermute(small, "pb", [(i, i ^ k) for i in range(b_n)]) for k in range(1, b_n)
    ]
    small = jnp.stack([small] + across_b, axis=1)
    gains = small[..., : 2 * norm_gains.shape[1]].reshape(rows_n, b_n, 2, -1)
    group = tok_seg.shape[0]
    seg_all = small[..., -2 * group : -group].astype(jnp.int32)
    pos_all = small[..., -group:].astype(jnp.int32)
    x_own = to_plane(block_input)
    x_group = row_gather(x_own)
    gains = untangle(untangle(gains, 0, z), 1, b).transpose(2, 0, 1, 3).reshape(2, width)
    gains = to_plane(gains)

    qkv_moved = turn(w_qkv)
    qkv_full = lax.all_gather(qkv_moved, PLANE, axis=1, tiled=True)
    out_moved = turn(after(w_out, x_group))
    out_full = lax.all_gather(out_moved, PLANE, axis=1, tiled=True)
    gate_up_moved = turn(after(w_gate_up, x_group))
    gate_up_full = lax.all_gather(gate_up_moved, PLANE, axis=1, tiled=True)
    down_moved = turn(after(w_down, gate_up_moved))
    down_full = lax.all_gather(down_moved, PLANE, axis=1, tiled=True)

    cot_own = to_plane(cotangent).astype(f32)
    grad_branch_f = row_gather(after((depth_scale * cot_own).astype(bf16), down_moved))

    pos_all = untangle(pos_all, 1, b).reshape(rows_n, b_n, x_n, c_n, own)
    seg_all = untangle(untangle(seg_all, 0, z), 1, b).reshape(pos_all.shape)
    index_all = jnp.arange(seg_all.size, dtype=jnp.int32).reshape(seg_all.shape)

    def for_group(array):
        array = lax.dynamic_slice_in_dim(array, b, 1, 1)
        array = lax.dynamic_slice_in_dim(array, x, 1, 2)
        return lax.dynamic_slice_in_dim(array, c, 1, 3).reshape(-1)

    def for_keys(array):
        array = untangle(array, 3, c).transpose(0, 3, 1, 2, 4)
        return array.reshape(-1, 8 * own)

    own_seg, own_index, pos_group = for_group(seg_all), for_group(index_all), for_group(pos_all)
    parent_seg, grand_seg = lineage(own_seg, seg_parent)
    query_info = jnp.stack([own_seg, parent_seg, grand_seg, own_index], axis=1)
    key_info = jnp.stack([for_keys(seg_all), for_keys(index_all)], axis=1)
    row = z.astype(jnp.int32).reshape(1)

    rows_a = x_group.astype(f32)
    normed_a = ((rows_a * inverse_rms(rows_a)) * gains[0]).astype(bf16)
    cosine, sine_table = rope_tables(pos_group)
    queries = (rotate(dot(normed_a, qkv_full[0]), cosine, sine_table)).astype(bf16) * bf16(HD**-0.5)
    keys = rotate(dot(normed_a, qkv_full[1]), cosine, sine_table).astype(bf16)
    values = dot(normed_a, qkv_full[2]).astype(bf16)
    queries = side_by_side(queries, None)
    kv = side_by_side(keys, values)
    chips = b_n * x_n
    kv = lax.all_to_all(jnp.broadcast_to(kv[None], (chips,) + kv.shape), CHIPS, 0, 0, tiled=True)
    kv = jnp.concatenate([kv, swap_core(kv)], axis=0).reshape(plane, rows_n, own, -1)
    saved = attend(row, query_info, key_info, queries, kv)
    attended = saved.reshape(rows_n * own, -1, 2, HD)[:, :, 1].reshape(rows_n * own, -1).astype(bf16)
    mid = x_own.astype(f32) + depth_scale * row_scatter(dot(attended, out_full))
    inv_f = inverse_rms(mid)
    unit_f = mid * inv_f
    normed_f = row_gather((unit_f * gains[1]).astype(bf16))
    gate = dot(normed_f, gate_up_full[0])
    up = dot(normed_f, gate_up_full[1])
    sig = jax.nn.sigmoid(gate)
    silu = gate * sig
    hidden = (silu * up).astype(bf16)
    output = mid + depth_scale * row_scatter(dot(hidden, down_full))

    grad_hidden = dot(grad_branch_f, down_full, ((1,), (1,)))
    grad_gate = (grad_hidden * up * sig * (1.0 + gate * (1.0 - sig))).astype(bf16)
    grad_up = (grad_hidden * silu).astype(bf16)
    grad_normed_f = row_scatter(
        dot(grad_gate, gate_up_full[0], ((1,), (1,))) + dot(grad_up, gate_up_full[1], ((1,), (1,)))
    )
    gain_f = jnp.sum(grad_normed_f * unit_f, axis=0)
    grad_mid = cot_own + norm_back(grad_normed_f * gains[1], unit_f, inv_f)
    grad_branch_a = row_gather((depth_scale * grad_mid).astype(bf16))

    grad_gate_up = jnp.stack([plane_scatter(normed_f, g) for g in (grad_gate, grad_up)])
    grad_down = plane_scatter(grad_branch_f, hidden)
    grad_out = plane_scatter(grad_branch_a, attended)
    grad_gate_up = turn(grad_gate_up).astype(f32)
    grad_down = turn(grad_down).astype(f32).T
    grad_out = turn(grad_out).astype(f32).T

    grad_attended = dot(grad_branch_a, out_full, ((1,), (1,))).astype(bf16)
    grad_q, grad_kv = attend_back(
        row, query_info, key_info, queries, kv, saved, side_by_side(None, grad_attended)
    )
    grad_kv = grad_kv.reshape(2, chips, rows_n * own, -1)
    grad_kv = (grad_kv[0].astype(f32) + swap_core(grad_kv[1]).astype(f32)).astype(bf16)
    grad_kv = lax.all_to_all(grad_kv, CHIPS, 0, 0, tiled=True)
    grad_kv = jnp.sum(grad_kv.astype(f32), axis=0).reshape(rows_n * own, -1, 2, HD)
    flat = (rows_n * own, w_qkv.shape[2])
    grad_q = grad_q.reshape(rows_n * own, -1, 2, HD)[:, :, 0].reshape(flat) * HD**-0.5
    grad_q = rotate(grad_q, cosine, -sine_table).astype(bf16)
    grad_k = rotate(grad_kv[:, :, 0].reshape(flat), cosine, -sine_table).astype(bf16)
    grad_v = grad_kv[:, :, 1].reshape(flat).astype(bf16)
    grad_normed_a = row_scatter(
        dot(grad_q, qkv_full[0], ((1,), (1,)))
        + dot(grad_k, qkv_full[1], ((1,), (1,)))
        + dot(grad_v, qkv_full[2], ((1,), (1,)))
    )
    grad_qkv = jnp.stack(
        [plane_scatter(normed_a, g) for g in (grad_q, grad_k, grad_v)]
    )
    grad_qkv = turn(grad_qkv).astype(f32)
    rows_own = x_own.astype(f32)
    inv_a = inverse_rms(rows_own)
    unit_a = rows_own * inv_a
    gain_a = jnp.sum(grad_normed_a * unit_a, axis=0)
    grad_input = grad_mid + norm_back(grad_normed_a * gains[0], unit_a, inv_a)
    gain_sum = from_plane(jnp.stack([gain_a, gain_f]))
    for axis, count in (("tc", c_n), ("tx", x_n), ("pb", b_n), ("za", rows_n)):
        for bit in range(count.bit_length() - 1):
            gain_sum = gain_sum + lax.ppermute(
                gain_sum, axis, [(i, i ^ (1 << bit)) for i in range(count)]
            )
    part = width // (rows_n * plane)
    place = ((z * b_n + b) * x_n + x) * c_n + c
    grad_gains = lax.dynamic_slice_in_dim(gain_sum, place * part, part, 1)
    return (from_plane(output), from_plane(grad_input), grad_qkv, grad_out, grad_gate_up, grad_down, grad_gains)


def solution(mesh):
    shares = mesh.shape["tensor"]
    devices = mesh.devices.reshape(shares, -1, shares // 2, 2)
    fine = Mesh(devices, ("za", "pb", "tx", "tc"))
    dp, tensor = ("za", "pb"), ("tx", "tc")
    in_specs = (
        P(dp + tensor, None),
        P(None, dp, tensor),
        P(tensor, dp),
        P(None, dp, tensor),
        P(tensor, dp),
        P(None, dp),
        P(dp + tensor, None),
        P(dp),
        P(dp),
        P(),
    )
    out_specs = (
        P(dp + tensor, None),
        P(dp + tensor, None),
        P(None, dp, tensor),
        P(tensor, dp),
        P(None, dp, tensor),
        P(tensor, dp),
        P(None, dp + tensor),
    )
    return jax.shard_map(
        on_device, mesh=fine, in_specs=in_specs, out_specs=out_specs, check_vma=False
    )
```

```python
import math

import jax
import jax.numpy as jnp
from jax import lax
from jax.experimental import pallas as pl
from jax.experimental.pallas import tpu as pltpu
from jax.sharding import Mesh, PartitionSpec as P

HD = 64

norm_eps = 1e-05
depth_scale = 1.4 / math.sqrt(40.0)
rope_base = 10000.0
far_below = -1e30
f32 = jnp.float32
bf16 = jnp.bfloat16

PLANE = ("tc", "tx", "pb")
CHIPS = ("tx", "pb")
ROW = "za"


def dot(a, b, dims=((1,), (0,))):
    return lax.dot_general(a, b, (dims, ((), ())), preferred_element_type=f32)


def send_row(array, distance):
    return lax.ppermute(array, ROW, [(i, i ^ distance) for i in range(lax.axis_size(ROW))])


def swap_core(array):
    return lax.ppermute(array, "tc", [(0, 1), (1, 0)])


def after(array, *done):
    return lax.optimization_barrier((array,) + done)[0]


def row_send(rows):
    return [rows] + [send_row(rows, k) for k in range(1, lax.axis_size(ROW))]


def row_split(partial):
    count = lax.axis_size(ROW)
    height = partial.shape[0] // count
    parts = [partial[k * height : (k + 1) * height] for k in range(count)]
    return [parts[0]] + [send_row(parts[k].astype(bf16), k) for k in range(1, count)]


def row_sum(parts):
    total = parts[0]
    for part in parts[1:]:
        total = total + part.astype(f32)
    return total


def halves(array, cut):
    return [array[:, :cut], array[:, cut:]]


def turn(parts, back=False):
    rows, shares = lax.axis_size(ROW), lax.axis_size("tx") * lax.axis_size("tc")

    def move(part, twist):
        pairs = [
            (z * shares + t, (t ^ twist) * shares + z % 2 * (shares // 2) + z // 2)
            for z in range(rows)
            for t in range(shares)
        ]
        if back:
            pairs = [(j, i) for i, j in pairs]
        return lax.ppermute(part, (ROW, "tx", "tc"), pairs)

    return [move(parts[0], 0), move(parts[1], shares // 2)]


def columns(parts):
    return jnp.concatenate(parts, axis=1)


def rows_of(parts):
    return jnp.concatenate(parts, axis=0)


def fence(*values):
    return lax.optimization_barrier(values)


def plane_gather(piece):
    return lax.all_gather(piece, PLANE, axis=0, tiled=True)


def with_twin(left):
    half = left.shape[1] // 2
    first = lax.axis_index("tc") == 0
    mine = jnp.where(first, left[:, :half], left[:, half:])
    other = jnp.where(first, left[:, half:], left[:, :half])
    return rows_of([mine, swap_core(other)])


def pair_sum(left, right):
    chips = lax.axis_size("pb") * lax.axis_size("tx")
    total = dot(rows_of([right, swap_core(right)]), left, ((0,), (0,))).astype(bf16).T
    return total.reshape(chips, -1, total.shape[1])


def exchange(blocks):
    return lax.all_to_all(blocks, CHIPS, 0, 0, tiled=True)


def chip_sum(received):
    return jnp.sum(received.astype(f32), axis=0).astype(bf16)


def lineage(segments, parents):
    seg_table = jnp.arange(parents.shape[0], dtype=jnp.int32)
    matches = segments[:, None] == seg_table[None, :]
    parent_seg = jnp.sum(jnp.where(matches, parents[None, :], 0), axis=1)
    matches = parent_seg[:, None] == seg_table[None, :]
    grand_seg = jnp.sum(jnp.where(matches, parents[None, :], 0), axis=1)
    grand_seg = jnp.where(parent_seg >= 0, grand_seg, -1)
    return (parent_seg, grand_seg)


def rope_tables(positions):
    half_size = HD // 2
    frequency = jnp.power(rope_base, -2.0 * jnp.arange(half_size, dtype=f32) / HD)
    angles = positions.astype(f32)[:, None] * frequency[None, :]
    return (jnp.cos(angles), jnp.sin(angles))


def rotate(flat, cosine, sine_table):
    values = flat.reshape(flat.shape[0], -1, HD)
    front = values[..., : HD // 2]
    latter = values[..., HD // 2 :]
    cos_rows = cosine[:, None, :]
    sin_rows = sine_table[:, None, :]
    return jnp.concatenate(
        [front * cos_rows - latter * sin_rows, latter * cos_rows + front * sin_rows], axis=-1
    ).reshape(flat.shape)


def norm_back(upstream, unit_rows, inv_rms):
    return inv_rms * (upstream - unit_rows * jnp.mean(upstream * unit_rows, axis=-1, keepdims=True))


def inverse_rms(rows):
    return lax.rsqrt(jnp.mean(rows * rows, axis=-1, keepdims=True) + norm_eps)


def heads_of(flat):
    return flat.reshape(flat.shape[0], -1, HD)


def side_by_side(left, right):
    count = (right if left is None else left).shape[0]
    parts = [None if t is None else heads_of(t) for t in (left, right)]
    blank = jnp.zeros_like(next(t for t in parts if t is not None))
    parts = [blank if t is None else t for t in parts]
    return jnp.concatenate(parts, axis=2).reshape(count, -1)


def fill_bias(query_ref, key_ref, bias_ref):
    @pl.when(pl.program_id(0) == 0)
    def _():
        seg, parent, grand, index = (query_ref[:, n : n + 1] for n in range(4))

        def fill(n, none):
            key_seg, key_index = key_ref[n, 0:1, :], key_ref[n, 1:2, :]
            allowed = (
                ((key_seg == seg) & (key_index <= index)) | (key_seg == parent) | (key_seg == grand)
            )
            bias_ref[n] = jnp.where(allowed, 0.0, far_below)
            return none

        lax.fori_loop(0, key_ref.shape[0], fill, 0)


def in_token_order(ref, row, chunks):
    height = ref.shape[0] // chunks
    return jnp.concatenate(
        [ref[pl.ds(pl.multiple_of((n ^ row) * height, 16), height), :] for n in range(chunks)], axis=0
    )


def keys_of(kv_ref, row, quarter, part, spans):
    count = kv_ref.shape[0] // spans
    block = kv_ref[pl.ds(part * count, count), quarter ^ row]
    return block.reshape(-1, 2 * HD)


def lower(top, change, skip):
    if skip == 0:
        return change(top)
    return jnp.concatenate([top[:skip], change(top[skip:])], axis=0)


def attend_kernel(row_ref, query_ref, key_ref, q_ref, kv_ref, out_ref, bias_ref):
    chunks, height = kv_ref.shape[1:3]
    spans = key_ref.shape[0] // chunks
    row = row_ref[0]
    fill_bias(query_ref, key_ref, bias_ref)
    q = in_token_order(q_ref, row, chunks)

    def span(part, carry):
        peak, total, mixed = carry
        keys = [keys_of(kv_ref, row, n, part, spans) for n in range(chunks)]
        scores = [
            dot(q[n * height :], keys[n], ((1,), (1,))) + bias_ref[n * spans + part, n * height :, :]
            for n in range(chunks)
        ]
        new_peak = peak
        for n in range(chunks):
            high = jnp.max(scores[n], axis=1, keepdims=True)
            new_peak = lower(new_peak, lambda p: jnp.maximum(p, high), n * height)
        factor = jnp.exp(peak - new_peak)
        total = total * factor
        mixed = mixed * factor
        for n in range(chunks):
            weights = jnp.exp(scores[n] - new_peak[n * height :])
            added = jnp.sum(weights, axis=1, keepdims=True)
            total = lower(total, lambda v: v + added, n * height)
            values = dot(weights.astype(bf16), keys[n])
            mixed = lower(mixed, lambda v: v + values, n * height)
        return new_peak, total, mixed

    start = (
        jnp.full((q.shape[0], 1), far_below, f32),
        jnp.zeros((q.shape[0], 1), f32),
        jnp.zeros((q.shape[0], 2 * HD), f32),
    )
    peak, total, mixed = span(0, start) if spans == 1 else lax.fori_loop(0, spans, span, start)
    lane = lax.broadcasted_iota(jnp.int32, mixed.shape, 1)
    result = jnp.where(lane < HD, peak + jnp.log(total), mixed / total)
    for n in range(chunks):
        out_ref[pl.ds(pl.multiple_of((n ^ row) * height, 16), height), :] = result[
            n * height : (n + 1) * height
        ]


def attend_back_kernel(
    row_ref, query_ref, key_ref, q_ref, kv_ref, out_ref, grad_ref, grad_q_ref, grad_kv_ref, bias_ref
):
    chunks, height = kv_ref.shape[1:3]
    spans = key_ref.shape[0] // chunks
    count = kv_ref.shape[0] // spans
    row = row_ref[0]
    fill_bias(query_ref, key_ref, bias_ref)
    q = in_token_order(q_ref, row, chunks)
    grad = in_token_order(grad_ref, row, chunks)
    saved = in_token_order(out_ref, row, chunks)
    log_total = saved[:, 0:1]
    delta = jnp.sum(grad.astype(f32) * saved, axis=1, keepdims=True)

    def span(part, grad_q):
        for n in range(chunks):
            skip = n * height
            keys = keys_of(kv_ref, row, n, part, spans)
            scores = dot(q[skip:], keys, ((1,), (1,))) + bias_ref[n * spans + part, skip:, :]
            probs = jnp.exp(scores - log_total[skip:])
            grad_probs = dot(grad[skip:], keys, ((1,), (1,)))
            grad_scores = (probs * (grad_probs - delta[skip:])).astype(bf16)
            added = dot(grad_scores, q[skip:], ((0,), (0,))) + dot(
                probs.astype(bf16), grad[skip:], ((0,), (0,))
            )
            grad_kv_ref[pl.ds(part * count, count), n ^ row] = added.astype(bf16).reshape(
                count, height, 2 * HD
            )
            more = dot(grad_scores, keys)
            grad_q = lower(grad_q, lambda v: v + more, skip)
        return grad_q

    start = jnp.zeros((q.shape[0], 2 * HD), f32)
    grad_q = span(0, start) if spans == 1 else lax.fori_loop(0, spans, span, start)
    for n in range(chunks):
        grad_q_ref[pl.ds(pl.multiple_of((n ^ row) * height, 16), height), :] = grad_q[
            n * height : (n + 1) * height
        ]


def attention_specs(queries, kv, query_info, key_info):
    heads = queries.shape[1] // (2 * HD)
    rows = pl.BlockSpec((queries.shape[0], 2 * HD), lambda h: (0, h))
    keys = pl.BlockSpec(kv.shape[:3] + (2 * HD,), lambda h: (0, 0, 0, h))
    fixed = [
        pl.BlockSpec(memory_space=pltpu.SMEM),
        pl.BlockSpec(query_info.shape, lambda h: (0, 0)),
        pl.BlockSpec(key_info.shape, lambda h: (0, 0, 0)),
    ]
    bias = pltpu.VMEM((key_info.shape[0], queries.shape[0], key_info.shape[2]), f32)
    params = pltpu.CompilerParams(vmem_limit_bytes=56 * 2**20)
    return heads, rows, keys, fixed, bias, params


def work(queries, kv, products):
    return pl.CostEstimate(
        flops=products * kv.size * 8000, bytes_accessed=4 * kv.size, transcendentals=0
    )


def attend(row, query_info, key_info, queries, kv):
    heads, rows, keys, fixed, bias, params = attention_specs(queries, kv, query_info, key_info)
    return pl.pallas_call(
        attend_kernel,
        grid=(heads,),
        in_specs=fixed + [rows, keys],
        out_specs=rows,
        out_shape=jax.ShapeDtypeStruct(queries.shape, f32),
        scratch_shapes=[bias],
        compiler_params=params,
        cost_estimate=work(queries, kv, 2),
    )(row, query_info, key_info, queries, kv)


def attend_back(row, query_info, key_info, queries, kv, saved, grad):
    heads, rows, keys, fixed, bias, params = attention_specs(queries, kv, query_info, key_info)
    return pl.pallas_call(
        attend_back_kernel,
        grid=(heads,),
        in_specs=fixed + [rows, keys, rows, rows],
        out_specs=[rows, keys],
        out_shape=[
            jax.ShapeDtypeStruct(queries.shape, f32),
            jax.ShapeDtypeStruct(kv.shape, bf16),
        ],
        scratch_shapes=[bias],
        compiler_params=params,
        cost_estimate=work(queries, kv, 5),
    )(row, query_info, key_info, queries, kv, saved, grad)


def on_device(
    block_input,
    w_qkv,
    w_out,
    w_gate_up,
    w_down,
    norm_gains,
    cotangent,
    tok_seg,
    tok_pos,
    seg_parent,
):
    rows_n, b_n, x_n, c_n = (lax.axis_size(n) for n in ("za", "pb", "tx", "tc"))
    z, b, x, c = (lax.axis_index(n) for n in ("za", "pb", "tx", "tc"))
    shares = x_n * c_n
    plane = b_n * shares
    own, width = block_input.shape
    piece = width // plane

    def untangle(array, axis, index):
        count = array.shape[axis]
        for bit in range(count.bit_length() - 1):
            step = 1 << bit
            shape = array.shape[:axis] + (count // (2 * step), 2, step) + array.shape[axis + 1 :]
            flipped = jnp.flip(array.reshape(shape), axis + 1).reshape(array.shape)
            array = jnp.where((index >> bit) & 1 == 1, flipped, array)
        return array

    features = w_qkv.shape[2]
    heads = features // HD
    near = (heads + 1) // 2
    units = w_down.shape[0]
    near_units = min(units, (units // 2 + 127) // 128 * 128)
    w_kv = side_by_side(w_qkv[1], w_qkv[2])

    low = 32
    small = jnp.concatenate(
        [norm_gains.reshape(-1)] + [t.astype(bf16) for t in (tok_seg, tok_pos // low, tok_pos % low)]
    )
    small = jnp.pad(small, (0, width - small.shape[0]))
    small = [small] + [
        lax.ppermute(small, "pb", [(i, i ^ k) for i in range(b_n)]) for k in range(1, b_n)
    ]
    kv_full = plane_gather(columns(turn(halves(w_kv, near * 2 * HD))))
    q_full = plane_gather(columns(turn(halves(w_qkv[0], near * HD))))
    x_own = block_input
    x_parts = row_send(jnp.concatenate([x_own, jnp.stack(small)], axis=0))
    x_parts, out_halves, gate_halves, up_halves, down_halves = fence(
        x_parts,
        halves(w_out.T, near * HD),
        halves(w_gate_up[0], near_units),
        halves(w_gate_up[1], near_units),
        halves(w_down.T, near_units),
    )
    out_moved = turn(out_halves)
    gate_moved = turn(gate_halves)
    small = jnp.stack([part[own:] for part in x_parts])
    gains = small[..., : 2 * norm_gains.shape[1]].reshape(rows_n, b_n, 2, -1)
    group = tok_seg.shape[0]
    small = small[..., gains.shape[3] * 2 :][..., : 3 * group].astype(jnp.int32)
    seg_all = small[..., :group]
    pos_all = small[..., group : 2 * group] * low + small[..., 2 * group :]
    gains = untangle(untangle(gains, 0, z), 1, b).transpose(2, 0, 1, 3).reshape(2, width)
    gains = gains.astype(f32)

    pos_all = untangle(pos_all, 1, b).reshape(rows_n, b_n, x_n, c_n, own)
    seg_all = untangle(untangle(seg_all, 0, z), 1, b).reshape(pos_all.shape)
    index_all = jnp.arange(seg_all.size, dtype=jnp.int32).reshape(seg_all.shape)

    def for_group(array):
        array = lax.dynamic_slice_in_dim(array, b, 1, 1)
        array = lax.dynamic_slice_in_dim(array, x, 1, 2)
        return lax.dynamic_slice_in_dim(array, c, 1, 3).reshape(-1)

    def for_keys(array):
        array = untangle(array, 3, c).transpose(0, 3, 2, 1, 4)
        return array.reshape(-1, 8 * own)

    own_seg, own_index, pos_group = for_group(seg_all), for_group(index_all), for_group(pos_all)
    parent_seg, grand_seg = lineage(own_seg, seg_parent)
    query_info = jnp.stack([own_seg, parent_seg, grand_seg, own_index], axis=1)
    key_info = jnp.stack([for_keys(seg_all), for_keys(index_all)], axis=1)
    row = z.astype(jnp.int32).reshape(1)

    cosine, sine_table = rope_tables(pos_group)
    cot_own = cotangent.astype(f32)
    branch_f = (depth_scale * cot_own).astype(bf16)
    rows_a = rows_of([part[:own] for part in x_parts]).astype(f32)
    normed_a = ((rows_a * inverse_rms(rows_a)) * gains[0]).astype(bf16)
    group = rows_n * own
    mine = dot(normed_a, kv_full).reshape(group, heads, 2, HD)
    keys = rotate(mine[:, :, 0].reshape(group, -1), cosine, sine_table).astype(bf16)
    mine = side_by_side(keys, mine[:, :, 1].reshape(group, -1).astype(bf16))
    mine, out_moved, gate_moved, up_halves, down_halves, branch_f = fence(
        mine, out_moved, gate_moved, up_halves, down_halves, branch_f
    )
    out_full = plane_gather(columns(out_moved))
    gate_full = plane_gather(columns(gate_moved))
    up_moved = turn(up_halves)
    down_moved = turn(down_halves)
    chips = b_n * x_n
    kv = exchange(jnp.broadcast_to(mine[None], (chips,) + mine.shape))
    queries = rotate(dot(after(normed_a, mine), q_full), cosine, sine_table)
    queries = side_by_side(queries.astype(bf16) * bf16(HD**-0.5), None)
    kv, up_moved, down_moved, queries, query_info, key_info, branch_f = fence(
        kv, up_moved, down_moved, queries, query_info, key_info, branch_f
    )
    up_full = plane_gather(columns(up_moved))
    down_full = plane_gather(columns(down_moved))
    f_parts = row_send(branch_f)
    kv = jnp.concatenate([kv, swap_core(kv)], axis=0).reshape(plane, rows_n, own, -1)
    saved = attend(row, query_info, key_info, queries, kv)
    attended = saved.reshape(group, heads, 2, HD)[:, :, 1].reshape(group, -1).astype(bf16)
    mid_part = dot(attended, out_full, ((1,), (1,)))
    parts = row_split(mid_part)
    parts, f_parts = fence(parts, f_parts)
    mid = x_own.astype(f32) + depth_scale * row_sum(parts)
    inv_f = inverse_rms(mid)
    unit_f = mid * inv_f
    normed_f = rows_of(row_send((unit_f * gains[1]).astype(bf16)))
    grad_branch_f = rows_of(f_parts)
    gate = dot(normed_f, gate_full)
    up = dot(normed_f, up_full)
    sig = jax.nn.sigmoid(gate)
    silu = gate * sig
    hidden = (silu * up).astype(bf16)
    gf_twin = with_twin(grad_branch_f)
    nf_twin = with_twin(normed_f)
    grad_hidden = dot(grad_branch_f, down_full)
    grad_gate = (grad_hidden * up * sig * (1.0 + gate * (1.0 - sig))).astype(bf16)
    grad_up = (grad_hidden * silu).astype(bf16)
    normed_part = dot(grad_gate, gate_full, ((1,), (1,))) + dot(grad_up, up_full, ((1,), (1,)))
    down_pair = pair_sum(gf_twin, hidden)
    normed_part, down_pair, hidden, grad_gate, grad_up, nf_twin = fence(
        normed_part, down_pair, hidden, grad_gate, grad_up, nf_twin
    )

    parts = row_split(normed_part)
    down_sum = exchange(down_pair)
    gate_pair = pair_sum(nf_twin, grad_gate)
    up_pair = pair_sum(nf_twin, grad_up)
    parts, down_sum, gate_pair, up_pair = fence(parts, down_sum, gate_pair, up_pair)
    grad_normed_f = row_sum(parts)
    gain_f = jnp.sum(grad_normed_f * unit_f, axis=0)
    grad_mid = cot_own + norm_back(grad_normed_f * gains[1], unit_f, inv_f)
    branch_a = (depth_scale * grad_mid).astype(bf16)

    parts = row_send(branch_a)
    gate_sum = exchange(gate_pair)
    down_sum = chip_sum(down_sum)
    parts, gate_sum, down_sum, up_pair = fence(parts, gate_sum, down_sum, up_pair)
    grad_branch_a = rows_of(parts)
    up_sum = exchange(up_pair)
    down_back = turn(halves(down_sum, near_units), True)
    gate_back = turn(halves(chip_sum(gate_sum), near_units), True)
    grad_attended = dot(grad_branch_a, out_full).astype(bf16)
    grad_q, grad_kv = attend_back(
        row, query_info, key_info, queries, kv, saved, side_by_side(None, grad_attended)
    )
    grad_q, grad_kv, up_sum, down_back, gate_back, hidden = fence(
        grad_q, grad_kv, up_sum, down_back, gate_back, hidden
    )

    output_part = dot(hidden, down_full, ((1,), (1,)))
    grad_kv = grad_kv.reshape(2, chips, group, -1)
    grad_kv = (grad_kv[0].astype(f32) + swap_core(grad_kv[1]).astype(f32)).astype(bf16)
    grad_kv, output_part = fence(grad_kv, output_part)
    grad_kv = exchange(grad_kv)
    output_parts = row_split(output_part)
    grad_q = grad_q.reshape(group, heads, 2, HD)[:, :, 0].reshape(group, -1) * HD**-0.5
    grad_q = rotate(grad_q, cosine, -sine_table).astype(bf16)
    q_pair = pair_sum(with_twin(normed_a), grad_q)
    out_pair = pair_sum(with_twin(grad_branch_a), attended)
    up_sum = chip_sum(up_sum)
    grad_kv, q_pair, out_pair, up_sum = fence(grad_kv, q_pair, out_pair, up_sum)
    grad_kv = jnp.sum(grad_kv.astype(f32), axis=0).reshape(group, heads, 2, HD)
    grad_k = rotate(grad_kv[:, :, 0].reshape(group, -1), cosine, -sine_table).astype(bf16)
    grad_kv = side_by_side(grad_k, grad_kv[:, :, 1].reshape(group, -1).astype(bf16))
    normed_part = dot(grad_q, q_full, ((1,), (1,))) + dot(grad_kv, kv_full, ((1,), (1,)))
    grad_kv, normed_part, output_parts = fence(grad_kv, normed_part, output_parts)
    two_sum = exchange(jnp.concatenate([q_pair, out_pair], axis=2))
    parts = row_split(normed_part)
    kv_pair = pair_sum(with_twin(normed_a), grad_kv)
    up_back = turn(halves(up_sum, near_units), True)
    kv_pair, two_sum, parts = fence(kv_pair, two_sum, parts)
    kv_sum = exchange(kv_pair)
    two_sum = chip_sum(two_sum)
    q_back = turn(halves(two_sum[:, :features], near * HD), True)
    out_back = turn(halves(two_sum[:, features:], near * HD), True)
    grad_normed_a = row_sum(parts)
    kv_back = turn(halves(chip_sum(kv_sum), near * 2 * HD), True)
    output = mid + depth_scale * row_sum(output_parts)

    grad_gate_up = jnp.stack([columns(gate_back), columns(up_back)]).astype(f32)
    grad_down = columns(down_back).astype(f32).T
    grad_out = columns(out_back).astype(f32).T
    grad_w_kv = columns(kv_back).reshape(piece, heads, 2, HD)
    grad_qkv = jnp.stack(
        [columns(q_back)] + [grad_w_kv[:, :, n].reshape(piece, features) for n in range(2)]
    ).astype(f32)
    rows_own = x_own.astype(f32)
    inv_a = inverse_rms(rows_own)
    unit_a = rows_own * inv_a
    gain_a = jnp.sum(grad_normed_a * unit_a, axis=0)
    grad_input = grad_mid + norm_back(grad_normed_a * gains[0], unit_a, inv_a)
    gain_sum = jnp.stack([gain_a, gain_f])
    for axis, count in (("tc", c_n), ("tx", x_n), ("pb", b_n), ("za", rows_n)):
        for bit in range(count.bit_length() - 1):
            gain_sum = gain_sum + lax.ppermute(
                gain_sum, axis, [(i, i ^ (1 << bit)) for i in range(count)]
            )
    part = width // (rows_n * plane)
    place = ((z * b_n + b) * x_n + x) * c_n + c
    grad_gains = lax.dynamic_slice_in_dim(gain_sum, place * part, part, 1)
    return (output, grad_input, grad_qkv, grad_out, grad_gate_up, grad_down, grad_gains)


def solution(mesh):
    shares = mesh.shape["tensor"]
    devices = mesh.devices.reshape(shares, -1, shares // 2, 2)
    fine = Mesh(devices, ("za", "pb", "tx", "tc"))
    dp, tensor = ("za", "pb"), ("tx", "tc")
    in_specs = (
        P(dp + tensor, None),
        P(None, dp, tensor),
        P(tensor, dp),
        P(None, dp, tensor),
        P(tensor, dp),
        P(None, dp),
        P(dp + tensor, None),
        P(dp),
        P(dp),
        P(),
    )
    out_specs = (
        P(dp + tensor, None),
        P(dp + tensor, None),
        P(None, dp, tensor),
        P(tensor, dp),
        P(None, dp, tensor),
        P(tensor, dp),
        P(None, dp + tensor),
    )
    return jax.shard_map(
        on_device, mesh=fine, in_specs=in_specs, out_specs=out_specs, check_vma=False
    )
```

```python
import math

import jax
import jax.numpy as jnp
from jax import lax
from jax.experimental import pallas as pl
from jax.experimental.pallas import tpu as pltpu
from jax.sharding import Mesh, PartitionSpec as P

HD = 64

norm_eps = 1e-05
depth_scale = 1.4 / math.sqrt(40.0)
rope_base = 10000.0
far_below = -1e30
f32 = jnp.float32
bf16 = jnp.bfloat16

PLANE = ("tc", "tx", "pb")
CHIPS = ("tx", "pb")
ROW = "za"


def dot(a, b, dims=((1,), (0,))):
    return lax.dot_general(a, b, (dims, ((), ())), preferred_element_type=f32)


def send_row(array, distance):
    return lax.ppermute(array, ROW, [(i, i ^ distance) for i in range(lax.axis_size(ROW))])


def swap_core(array):
    return lax.ppermute(array, "tc", [(0, 1), (1, 0)])


def after(array, *done):
    return lax.optimization_barrier((array,) + done)[0]


def row_send(rows):
    return [rows] + [send_row(rows, k) for k in range(1, lax.axis_size(ROW))]


def row_split(partial):
    count = lax.axis_size(ROW)
    height = partial.shape[0] // count
    parts = [partial[k * height : (k + 1) * height] for k in range(count)]
    return [parts[0]] + [send_row(parts[k].astype(bf16), k) for k in range(1, count)]


def row_sum(parts):
    total = parts[0]
    for part in parts[1:]:
        total = total + part.astype(f32)
    return total


def bundle(arrays, cuts):
    return [
        columns([a[:, :cut] for a, cut in zip(arrays, cuts)]),
        columns([a[:, cut:] for a, cut in zip(arrays, cuts)]),
    ]


def unbundle(parts, widths, cuts):
    arrays, first, second = [], 0, 0
    for wide, cut in zip(widths, cuts):
        rest = wide - cut
        arrays.append(columns([parts[0][:, first : first + cut], parts[1][:, second : second + rest]]))
        first, second = first + cut, second + rest
    return arrays


def turn(parts, back=False):
    rows, shares = lax.axis_size(ROW), lax.axis_size("tx") * lax.axis_size("tc")

    def move(part, twist):
        pairs = [
            (z * shares + t, (t ^ twist) * shares + z % 2 * (shares // 2) + z // 2)
            for z in range(rows)
            for t in range(shares)
        ]
        if back:
            pairs = [(j, i) for i, j in pairs]
        return lax.ppermute(part, (ROW, "tx", "tc"), pairs)

    return [move(parts[0], 0), move(parts[1], shares // 2)]


def columns(parts):
    return jnp.concatenate(parts, axis=1)


def rows_of(parts):
    return jnp.concatenate(parts, axis=0)


def fence(*values):
    return lax.optimization_barrier(values)


def plane_gather(piece):
    return lax.all_gather(piece, PLANE, axis=0, tiled=True)


def core_halves(array):
    half = array.shape[1] // 2
    first = lax.axis_index("tc") == 0
    left, right = array[:, :half], array[:, half:]
    return jnp.where(first, left, right), jnp.where(first, right, left)


def with_twin(left):
    mine, other = core_halves(left)
    return [mine, swap_core(other)]


def pair_kernel(left_ref, left_far_ref, right_ref, right_far_ref, out_ref):
    total = dot(left_ref[...], right_ref[...], ((0,), (0,)))
    total += dot(left_far_ref[...], right_far_ref[...], ((0,), (0,)))
    out_ref[...] = total.astype(bf16)


def pair_sum(left, right):
    chips = lax.axis_size("pb") * lax.axis_size("tx")
    tokens, rows = left[0].shape
    wide = right.shape[1]
    tile = 384 if rows % 384 == 0 else rows
    lefts = pl.BlockSpec((tokens, tile), lambda i: (0, i))
    rights = pl.BlockSpec((tokens, wide), lambda i: (0, 0))
    total = pl.pallas_call(
        pair_kernel,
        grid=(rows // tile,),
        in_specs=[lefts, lefts, rights, rights],
        out_specs=pl.BlockSpec((tile, wide), lambda i: (i, 0)),
        out_shape=jax.ShapeDtypeStruct((rows, wide), bf16),
        compiler_params=pltpu.CompilerParams(vmem_limit_bytes=40 * 2**20),
        cost_estimate=pl.CostEstimate(
            flops=4 * tokens * rows * wide, bytes_accessed=2 * rows * wide, transcendentals=0
        ),
    )(*left, right, swap_core(right))
    return total.reshape(chips, -1, wide)


def exchange(blocks):
    return lax.all_to_all(blocks, CHIPS, 0, 0, tiled=True)


def chip_sum(received):
    return jnp.sum(received.astype(f32), axis=0).astype(bf16)


def lineage(segments, parents):
    seg_table = jnp.arange(parents.shape[0], dtype=jnp.int32)
    matches = segments[:, None] == seg_table[None, :]
    parent_seg = jnp.sum(jnp.where(matches, parents[None, :], 0), axis=1)
    matches = parent_seg[:, None] == seg_table[None, :]
    grand_seg = jnp.sum(jnp.where(matches, parents[None, :], 0), axis=1)
    grand_seg = jnp.where(parent_seg >= 0, grand_seg, -1)
    return (parent_seg, grand_seg)


def rope_tables(positions):
    half_size = HD // 2
    frequency = jnp.power(rope_base, -2.0 * jnp.arange(half_size, dtype=f32) / HD)
    angles = positions.astype(f32)[:, None] * frequency[None, :]
    return (jnp.cos(angles), jnp.sin(angles))


def rotate(flat, cosine, sine_table):
    values = flat.reshape(flat.shape[0], -1, HD)
    front = values[..., : HD // 2]
    latter = values[..., HD // 2 :]
    cos_rows = cosine[:, None, :]
    sin_rows = sine_table[:, None, :]
    return jnp.concatenate(
        [front * cos_rows - latter * sin_rows, latter * cos_rows + front * sin_rows], axis=-1
    ).reshape(flat.shape)


def norm_back(upstream, unit_rows, inv_rms):
    return inv_rms * (upstream - unit_rows * jnp.mean(upstream * unit_rows, axis=-1, keepdims=True))


def inverse_rms(rows):
    return lax.rsqrt(jnp.mean(rows * rows, axis=-1, keepdims=True) + norm_eps)


def heads_of(flat):
    return flat.reshape(flat.shape[0], -1, HD)


def side_by_side(left, right):
    count = (right if left is None else left).shape[0]
    parts = [None if t is None else heads_of(t) for t in (left, right)]
    blank = jnp.zeros_like(next(t for t in parts if t is not None))
    parts = [blank if t is None else t for t in parts]
    return jnp.concatenate(parts, axis=2).reshape(count, -1)


def fill_bias(query_ref, key_ref, bias_ref):
    @pl.when(pl.program_id(0) == 0)
    def _():
        seg, parent, grand, index = (query_ref[:, n : n + 1] for n in range(4))

        def fill(n, none):
            key_seg, key_index = key_ref[n, 0:1, :], key_ref[n, 1:2, :]
            allowed = (
                ((key_seg == seg) & (key_index <= index)) | (key_seg == parent) | (key_seg == grand)
            )
            bias_ref[n] = jnp.where(allowed, 0.0, far_below)
            return none

        lax.fori_loop(0, key_ref.shape[0], fill, 0)


def in_token_order(ref, row, chunks):
    height = ref.shape[0] // chunks
    return jnp.concatenate(
        [ref[pl.ds(pl.multiple_of((n ^ row) * height, 16), height), :] for n in range(chunks)], axis=0
    )


def span_of(refs, row, quarter, part, count):
    where = (pl.ds(part * count, count), quarter ^ row)
    return rows_of([ref[where].reshape(-1, 2 * HD) for ref in refs])


def lower(top, change, skip):
    if skip == 0:
        return change(top)
    return jnp.concatenate([top[:skip], change(top[skip:])], axis=0)


def attend_kernel(row_ref, query_ref, key_ref, q_ref, near_ref, far_ref, out_ref, bias_ref):
    chips, chunks, height = near_ref.shape[:3]
    spans = key_ref.shape[0] // chunks
    count = chips // spans
    row = row_ref[0]
    fill_bias(query_ref, key_ref, bias_ref)
    q = in_token_order(q_ref, row, chunks)

    def span(part, carry):
        peak, total, mixed = carry
        keys = [span_of((near_ref, far_ref), row, n, part, count) for n in range(chunks)]
        scores = [
            dot(q[n * height :], keys[n], ((1,), (1,))) + bias_ref[n * spans + part, n * height :, :]
            for n in range(chunks)
        ]
        new_peak = peak
        for n in range(chunks):
            high = jnp.max(scores[n], axis=1, keepdims=True)
            new_peak = lower(new_peak, lambda p: jnp.maximum(p, high), n * height)
        factor = jnp.exp(peak - new_peak)
        total = total * factor
        mixed = mixed * factor
        for n in range(chunks):
            weights = jnp.exp(scores[n] - new_peak[n * height :])
            added = jnp.sum(weights, axis=1, keepdims=True)
            total = lower(total, lambda v: v + added, n * height)
            values = dot(weights.astype(bf16), keys[n])
            mixed = lower(mixed, lambda v: v + values, n * height)
        return new_peak, total, mixed

    start = (
        jnp.full((q.shape[0], 1), far_below, f32),
        jnp.zeros((q.shape[0], 1), f32),
        jnp.zeros((q.shape[0], 2 * HD), f32),
    )
    peak, total, mixed = span(0, start) if spans == 1 else lax.fori_loop(0, spans, span, start)
    lane = lax.broadcasted_iota(jnp.int32, mixed.shape, 1)
    result = jnp.where(lane < HD, peak + jnp.log(total), mixed / total)
    for n in range(chunks):
        out_ref[pl.ds(pl.multiple_of((n ^ row) * height, 16), height), :] = result[
            n * height : (n + 1) * height
        ]


def attend_back_kernel(
    row_ref,
    query_ref,
    key_ref,
    q_ref,
    near_ref,
    far_ref,
    out_ref,
    grad_ref,
    grad_q_ref,
    grad_near_ref,
    grad_far_ref,
    bias_ref,
):
    chips, chunks, height = near_ref.shape[:3]
    spans = key_ref.shape[0] // chunks
    count = chips // spans
    row = row_ref[0]
    fill_bias(query_ref, key_ref, bias_ref)
    q = in_token_order(q_ref, row, chunks)
    grad = in_token_order(grad_ref, row, chunks)
    saved = in_token_order(out_ref, row, chunks)
    log_total = saved[:, 0:1]
    delta = jnp.sum(grad.astype(f32) * saved, axis=1, keepdims=True)

    def span(part, grad_q):
        for n in range(chunks):
            skip = n * height
            keys = span_of((near_ref, far_ref), row, n, part, count)
            scores = dot(q[skip:], keys, ((1,), (1,))) + bias_ref[n * spans + part, skip:, :]
            probs = jnp.exp(scores - log_total[skip:])
            grad_probs = dot(grad[skip:], keys, ((1,), (1,)))
            grad_scores = (probs * (grad_probs - delta[skip:])).astype(bf16)
            added = dot(grad_scores, q[skip:], ((0,), (0,))) + dot(
                probs.astype(bf16), grad[skip:], ((0,), (0,))
            )
            added = added.astype(bf16).reshape(2, count, height, 2 * HD)
            where = (pl.ds(part * count, count), n ^ row)
            grad_near_ref[where] = added[0]
            grad_far_ref[where] = added[1]
            more = dot(grad_scores, keys)
            grad_q = lower(grad_q, lambda v: v + more, skip)
        return grad_q

    start = jnp.zeros((q.shape[0], 2 * HD), f32)
    grad_q = span(0, start) if spans == 1 else lax.fori_loop(0, spans, span, start)
    for n in range(chunks):
        grad_q_ref[pl.ds(pl.multiple_of((n ^ row) * height, 16), height), :] = grad_q[
            n * height : (n + 1) * height
        ]


def attention_specs(queries, kv, query_info, key_info):
    heads = queries.shape[1] // (2 * HD)
    rows = pl.BlockSpec((queries.shape[0], 2 * HD), lambda h: (0, h))
    keys = pl.BlockSpec(kv[0].shape[:3] + (2 * HD,), lambda h: (0, 0, 0, h))
    fixed = [
        pl.BlockSpec(memory_space=pltpu.SMEM),
        pl.BlockSpec(query_info.shape, lambda h: (0, 0)),
        pl.BlockSpec(key_info.shape, lambda h: (0, 0, 0)),
    ]
    bias = pltpu.VMEM((key_info.shape[0], queries.shape[0], key_info.shape[2]), f32)
    params = pltpu.CompilerParams(vmem_limit_bytes=56 * 2**20)
    return heads, rows, keys, fixed, bias, params


def work(kv, products):
    return pl.CostEstimate(
        flops=products * kv[0].size * 16000, bytes_accessed=8 * kv[0].size, transcendentals=0
    )


def attend(row, query_info, key_info, queries, kv):
    heads, rows, keys, fixed, bias, params = attention_specs(queries, kv, query_info, key_info)
    return pl.pallas_call(
        attend_kernel,
        grid=(heads,),
        in_specs=fixed + [rows, keys, keys],
        out_specs=rows,
        out_shape=jax.ShapeDtypeStruct(queries.shape, f32),
        scratch_shapes=[bias],
        compiler_params=params,
        cost_estimate=work(kv, 2),
    )(row, query_info, key_info, queries, *kv)


def attend_back(row, query_info, key_info, queries, kv, saved, grad):
    heads, rows, keys, fixed, bias, params = attention_specs(queries, kv, query_info, key_info)
    return pl.pallas_call(
        attend_back_kernel,
        grid=(heads,),
        in_specs=fixed + [rows, keys, keys, rows, rows],
        out_specs=[rows, keys, keys],
        out_shape=[jax.ShapeDtypeStruct(queries.shape, f32)]
        + [jax.ShapeDtypeStruct(t.shape, bf16) for t in kv],
        scratch_shapes=[bias],
        compiler_params=params,
        cost_estimate=work(kv, 5),
    )(row, query_info, key_info, queries, *kv, saved, grad)


def on_device(
    block_input,
    w_qkv,
    w_out,
    w_gate_up,
    w_down,
    norm_gains,
    cotangent,
    tok_seg,
    tok_pos,
    seg_parent,
):
    rows_n, b_n, x_n, c_n = (lax.axis_size(n) for n in ("za", "pb", "tx", "tc"))
    z, b, x, c = (lax.axis_index(n) for n in ("za", "pb", "tx", "tc"))
    shares = x_n * c_n
    plane = b_n * shares
    own, width = block_input.shape
    piece = width // plane

    def untangle(array, axis, index):
        count = array.shape[axis]
        for bit in range(count.bit_length() - 1):
            step = 1 << bit
            shape = array.shape[:axis] + (count // (2 * step), 2, step) + array.shape[axis + 1 :]
            flipped = jnp.flip(array.reshape(shape), axis + 1).reshape(array.shape)
            array = jnp.where((index >> bit) & 1 == 1, flipped, array)
        return array

    features = w_qkv.shape[2]
    heads = features // HD
    near = (heads + 1) // 2
    units = w_down.shape[0]
    near_units = min(units, (units // 2 + 127) // 128 * 128)
    w_kv = side_by_side(w_qkv[1], w_qkv[2])

    low = 32
    small = jnp.concatenate(
        [norm_gains.reshape(-1)] + [t.astype(bf16) for t in (tok_seg, tok_pos // low, tok_pos % low)]
    )
    small = jnp.pad(small, (0, width - small.shape[0]))[None]
    x_own = block_input
    x_parts = row_send(rows_of([x_own, small]))
    kv_full = plane_gather(*unbundle(turn(bundle([w_kv], [near * 2 * HD])), [2 * features], [near * 2 * HD]))
    q_full = plane_gather(*unbundle(turn(bundle([w_qkv[0]], [near * HD])), [features], [near * HD]))
    first = bundle([w_gate_up[0], w_gate_up[1], w_out.T], [near_units, near_units, near * HD])
    second = bundle([w_down.T], [near_units])
    x_parts, first, second = fence(x_parts, first, second)
    first = turn(first)
    small = rows_of([part[own:] for part in x_parts])
    small = [small] + [
        lax.ppermute(small, "pb", [(i, i ^ k) for i in range(b_n)]) for k in range(1, b_n)
    ]
    small = jnp.stack(small, axis=1)
    gains = small[..., : 2 * norm_gains.shape[1]].reshape(rows_n, b_n, 2, -1)
    group = tok_seg.shape[0]
    small = small[..., gains.shape[3] * 2 :][..., : 3 * group].astype(jnp.int32)
    seg_all = small[..., :group]
    pos_all = small[..., group : 2 * group] * low + small[..., 2 * group :]
    gains = untangle(untangle(gains, 0, z), 1, b).transpose(2, 0, 1, 3).reshape(2, width)
    gains = gains.astype(f32)

    pos_all = untangle(pos_all, 1, b).reshape(rows_n, b_n, x_n, c_n, own)
    seg_all = untangle(untangle(seg_all, 0, z), 1, b).reshape(pos_all.shape)
    index_all = jnp.arange(seg_all.size, dtype=jnp.int32).reshape(seg_all.shape)

    def for_group(array):
        array = lax.dynamic_slice_in_dim(array, b, 1, 1)
        array = lax.dynamic_slice_in_dim(array, x, 1, 2)
        return lax.dynamic_slice_in_dim(array, c, 1, 3).reshape(-1)

    def for_keys(array):
        array = untangle(array, 3, c).transpose(0, 3, 2, 1, 4).reshape(rows_n, 2, -1, 4, own)
        return array.transpose(0, 2, 1, 3, 4).reshape(-1, 8 * own)

    own_seg, own_index, pos_group = for_group(seg_all), for_group(index_all), for_group(pos_all)
    parent_seg, grand_seg = lineage(own_seg, seg_parent)
    query_info = jnp.stack([own_seg, parent_seg, grand_seg, own_index], axis=1)
    key_info = jnp.stack([for_keys(seg_all), for_keys(index_all)], axis=1)
    row = z.astype(jnp.int32).reshape(1)

    cosine, sine_table = rope_tables(pos_group)
    cot_own = cotangent.astype(f32)
    branch_f = (depth_scale * cot_own).astype(bf16)
    rows_a = rows_of([part[:own] for part in x_parts]).astype(f32)
    normed_a = ((rows_a * inverse_rms(rows_a)) * gains[0]).astype(bf16)
    group = rows_n * own
    mine = dot(normed_a, kv_full).reshape(group, heads, 2, HD)
    keys = rotate(mine[:, :, 0].reshape(group, -1), cosine, sine_table).astype(bf16)
    mine = side_by_side(keys, mine[:, :, 1].reshape(group, -1).astype(bf16))
    mine, second, branch_f, query_info, key_info = fence(
        mine, second, branch_f, query_info, key_info
    )
    gate_moved, up_moved, out_moved = unbundle(
        after(first, mine), [units, units, features], [near_units, near_units, near * HD]
    )
    out_full, gate_full, up_full = plane_gather(out_moved), plane_gather(gate_moved), plane_gather(up_moved)
    second = turn(second)
    f_parts = row_send(branch_f)
    chips = b_n * x_n
    kv = exchange(jnp.broadcast_to(mine[None], (chips,) + mine.shape))
    queries = rotate(dot(after(normed_a, mine), q_full), cosine, sine_table)
    queries = side_by_side(queries.astype(bf16) * bf16(HD**-0.5), None)
    kv, second, queries, f_parts = fence(kv, second, queries, f_parts)
    (down_moved,) = unbundle(second, [units], [near_units])
    kv = [t.reshape(chips, rows_n, own, -1) for t in (kv, swap_core(kv))]
    saved = attend(row, query_info, key_info, queries, kv)
    attended = saved.reshape(group, heads, 2, HD)[:, :, 1].reshape(group, -1).astype(bf16)
    mid_part = dot(attended, out_full, ((1,), (1,)))
    parts = row_split(mid_part)
    down_near = exchange(jnp.broadcast_to(down_moved[None], (chips,) + down_moved.shape))
    parts, down_near = fence(parts, down_near)
    down_near = down_near.reshape(-1, units)
    down_full = rows_of([down_near, swap_core(down_near)])
    mid = x_own.astype(f32) + depth_scale * row_sum(parts)
    inv_f = inverse_rms(mid)
    unit_f = mid * inv_f
    normed_f = rows_of(row_send((unit_f * gains[1]).astype(bf16)))
    grad_branch_f = rows_of(f_parts)
    gate = dot(normed_f, gate_full)
    up = dot(normed_f, up_full)
    sig = jax.nn.sigmoid(gate)
    silu = gate * sig
    hidden = (silu * up).astype(bf16)
    gf_twin = with_twin(grad_branch_f)
    nf_twin = with_twin(normed_f)
    grad_hidden = dot(columns(core_halves(grad_branch_f)), down_full)
    grad_gate = (grad_hidden * up * sig * (1.0 + gate * (1.0 - sig))).astype(bf16)
    grad_up = (grad_hidden * silu).astype(bf16)
    normed_part = dot(grad_gate, gate_full, ((1,), (1,))) + dot(grad_up, up_full, ((1,), (1,)))
    down_pair = pair_sum(gf_twin, hidden)
    normed_part, down_pair, hidden, grad_gate, grad_up, nf_twin = fence(
        normed_part, down_pair, hidden, grad_gate, grad_up, nf_twin
    )

    parts = row_split(normed_part)
    down_sum = exchange(down_pair)
    gate_pair = pair_sum(nf_twin, grad_gate)
    up_pair = pair_sum(nf_twin, grad_up)
    parts, down_sum, gate_pair, up_pair = fence(parts, down_sum, gate_pair, up_pair)
    grad_normed_f = row_sum(parts)
    gain_f = jnp.sum(grad_normed_f * unit_f, axis=0)
    grad_mid = cot_own + norm_back(grad_normed_f * gains[1], unit_f, inv_f)
    branch_a = (depth_scale * grad_mid).astype(bf16)

    parts = row_send(branch_a)
    gate_sum = exchange(gate_pair)
    down_sum = chip_sum(down_sum)
    output_part = dot(after(hidden, branch_a), down_full, ((1,), (1,)))
    na_twin = with_twin(after(normed_a, branch_a))
    attended = after(attended, branch_a)
    parts, gate_sum, down_sum, up_pair, output_part, na_twin, attended = fence(
        parts, gate_sum, down_sum, up_pair, output_part, na_twin, attended
    )
    two_back = bundle([down_sum, chip_sum(gate_sum)], [near_units, near_units])
    grad_branch_a = rows_of(parts)
    up_sum = exchange(up_pair)
    output_parts = row_split(output_part)
    grad_attended = dot(grad_branch_a, out_full).astype(bf16)
    grad_q, *grad_kv = attend_back(
        row, query_info, key_info, queries, kv, saved, side_by_side(None, grad_attended)
    )
    grad_q, grad_kv, up_sum, output_parts = fence(grad_q, grad_kv, up_sum, output_parts)

    grad_kv = (grad_kv[0].astype(f32) + swap_core(grad_kv[1]).astype(f32)).astype(bf16)
    grad_kv = grad_kv.reshape(chips, group, -1)
    grad_kv, grad_q, up_sum, two_back, grad_branch_a = fence(
        grad_kv, grad_q, up_sum, two_back, grad_branch_a
    )
    grad_kv = exchange(grad_kv)
    two_back = turn(two_back, True)
    up_back = bundle([chip_sum(up_sum)], [near_units])
    grad_q = grad_q.reshape(group, heads, 2, HD)[:, :, 0].reshape(group, -1) * HD**-0.5
    grad_q = rotate(grad_q, cosine, -sine_table).astype(bf16)
    q_pair = pair_sum(na_twin, grad_q)
    out_pair = pair_sum(with_twin(grad_branch_a), attended)
    two_pair = jnp.concatenate([q_pair, out_pair], axis=2)
    grad_kv, two_pair = fence(grad_kv, two_pair)
    two_sum = exchange(two_pair)
    grad_kv = jnp.sum(grad_kv.astype(f32), axis=0).reshape(group, heads, 2, HD)
    grad_k = rotate(grad_kv[:, :, 0].reshape(group, -1), cosine, -sine_table).astype(bf16)
    grad_kv = side_by_side(grad_k, grad_kv[:, :, 1].reshape(group, -1).astype(bf16))
    normed_part = dot(grad_q, q_full, ((1,), (1,))) + dot(grad_kv, kv_full, ((1,), (1,)))
    grad_kv, normed_part, two_back, up_back = fence(grad_kv, normed_part, two_back, up_back)
    parts = row_split(normed_part)
    kv_pair = pair_sum(na_twin, grad_kv)
    kv_pair, two_sum = fence(kv_pair, two_sum)
    kv_sum = exchange(kv_pair)
    two_sum = chip_sum(two_sum)
    parts, two_sum, up_back = fence(parts, two_sum, up_back)
    up_back = turn(up_back, True)
    grad_normed_a = row_sum(parts)
    output = mid + depth_scale * columns(core_halves(row_sum(output_parts)))
    kv_sum, up_back = fence(kv_sum, up_back)
    last_cuts = [near * 2 * HD, near * HD, near * HD]
    last_back = bundle([chip_sum(kv_sum), two_sum[:, :features], two_sum[:, features:]], last_cuts)
    last_back = turn(last_back, True)

    grad_w_down, grad_w_gate = unbundle(two_back, [units, units], [near_units, near_units])
    (grad_w_up,) = unbundle(up_back, [units], [near_units])
    grad_w_kv, grad_w_q, grad_w_out = unbundle(last_back, [2 * features, features, features], last_cuts)
    grad_gate_up = jnp.stack([grad_w_gate, grad_w_up]).astype(f32)
    grad_down = grad_w_down.astype(f32).T
    grad_out = grad_w_out.astype(f32).T
    grad_w_kv = grad_w_kv.reshape(piece, heads, 2, HD)
    grad_qkv = jnp.stack(
        [grad_w_q] + [grad_w_kv[:, :, n].reshape(piece, features) for n in range(2)]
    ).astype(f32)
    rows_own = x_own.astype(f32)
    inv_a = inverse_rms(rows_own)
    unit_a = rows_own * inv_a
    gain_a = jnp.sum(grad_normed_a * unit_a, axis=0)
    grad_input = grad_mid + norm_back(grad_normed_a * gains[0], unit_a, inv_a)
    gain_sum = jnp.stack([gain_a, gain_f])
    for axis, count in (("tc", c_n), ("tx", x_n), ("pb", b_n), ("za", rows_n)):
        for bit in range(count.bit_length() - 1):
            gain_sum = gain_sum + lax.ppermute(
                gain_sum, axis, [(i, i ^ (1 << bit)) for i in range(count)]
            )
    part = width // (rows_n * plane)
    place = ((z * b_n + b) * x_n + x) * c_n + c
    grad_gains = lax.dynamic_slice_in_dim(gain_sum, place * part, part, 1)
    return (output, grad_input, grad_qkv, grad_out, grad_gate_up, grad_down, grad_gains)


def solution(mesh):
    shares = mesh.shape["tensor"]
    devices = mesh.devices.reshape(shares, -1, shares // 2, 2)
    fine = Mesh(devices, ("za", "pb", "tx", "tc"))
    dp, tensor = ("za", "pb"), ("tx", "tc")
    in_specs = (
        P(dp + tensor, None),
        P(None, dp, tensor),
        P(tensor, dp),
        P(None, dp, tensor),
        P(tensor, dp),
        P(None, dp),
        P(dp + tensor, None),
        P(dp),
        P(dp),
        P(),
    )
    out_specs = (
        P(dp + tensor, None),
        P(dp + tensor, None),
        P(None, dp, tensor),
        P(tensor, dp),
        P(None, dp, tensor),
        P(tensor, dp),
        P(None, dp + tensor),
    )
    return jax.shard_map(
        on_device, mesh=fine, in_specs=in_specs, out_specs=out_specs, check_vma=False
    )
```

```python
import math

import jax
import jax.numpy as jnp
from jax import lax
from jax.experimental import pallas as pl
from jax.experimental.pallas import tpu as pltpu
from jax.sharding import Mesh, PartitionSpec as P

HD = 64

norm_eps = 1e-05
depth_scale = 1.4 / math.sqrt(40.0)
rope_base = 10000.0
far_below = -1e30
f32 = jnp.float32
bf16 = jnp.bfloat16

PLANE = ("tc", "tx", "pb")
CHIPS = ("tx", "pb")
ROW = "za"


def dot(a, b, dims=((1,), (0,))):
    return lax.dot_general(a, b, (dims, ((), ())), preferred_element_type=f32)


def send_row(array, distance):
    return lax.ppermute(array, ROW, [(i, i ^ distance) for i in range(lax.axis_size(ROW))])


def swap_core(array):
    return lax.ppermute(array, "tc", [(0, 1), (1, 0)])


def after(array, *done):
    return lax.optimization_barrier((array,) + done)[0]


def row_send(rows):
    count = lax.axis_size(ROW)
    if count != 4:
        return [rows] + [send_row(rows, k) for k in range(1, count)]
    side, across = send_row(rows, 1), send_row(rows, 2)
    return [rows, side, across, send_row(across, 1)]


def row_split(partial):
    count = lax.axis_size(ROW)
    height = partial.shape[0] // count
    parts = [partial[k * height : (k + 1) * height] for k in range(count)]
    if count != 4:
        return [parts[0]] + [send_row(parts[k].astype(bf16), k) for k in range(1, count)]
    far = send_row(parts[3].astype(bf16), 1)
    return [
        parts[0],
        send_row(parts[1].astype(bf16), 1),
        send_row((parts[2] + far.astype(f32)).astype(bf16), 2),
    ]


def row_sum(parts):
    total = parts[0]
    for part in parts[1:]:
        total = total + part.astype(f32)
    return total


def bundle(arrays, cuts):
    return [
        columns([a[:, :cut] for a, cut in zip(arrays, cuts)]),
        columns([a[:, cut:] for a, cut in zip(arrays, cuts)]),
    ]


def unbundle(parts, widths, cuts):
    arrays, first, second = [], 0, 0
    for wide, cut in zip(widths, cuts):
        rest = wide - cut
        arrays.append(columns([parts[0][:, first : first + cut], parts[1][:, second : second + rest]]))
        first, second = first + cut, second + rest
    return arrays


def turn(parts, back=False):
    rows, shares = lax.axis_size(ROW), lax.axis_size("tx") * lax.axis_size("tc")

    def move(part, twist):
        pairs = [
            (z * shares + t, (t ^ twist) * shares + z % 2 * (shares // 2) + z // 2)
            for z in range(rows)
            for t in range(shares)
        ]
        if back:
            pairs = [(j, i) for i, j in pairs]
        return lax.ppermute(part, (ROW, "tx", "tc"), pairs)

    return [move(parts[0], 0), move(parts[1], shares // 2)]


def columns(parts):
    return jnp.concatenate(parts, axis=1)


def rows_of(parts):
    return jnp.concatenate(parts, axis=0)


def fence(*values):
    return lax.optimization_barrier(values)


def plane_gather(piece):
    return lax.all_gather(piece, PLANE, axis=0, tiled=True)


def core_halves(array):
    half = array.shape[1] // 2
    first = lax.axis_index("tc") == 0
    left, right = array[:, :half], array[:, half:]
    return jnp.where(first, left, right), jnp.where(first, right, left)


def with_twin(left):
    mine, other = core_halves(left)
    return [mine, swap_core(other)]


def pair_kernel(left_ref, left_far_ref, right_ref, right_far_ref, out_ref):
    total = dot(left_ref[...], right_ref[...], ((0,), (0,)))
    total += dot(left_far_ref[...], right_far_ref[...], ((0,), (0,)))
    out_ref[...] = total.astype(bf16)


def pair_sum(left, right):
    chips = lax.axis_size("pb") * lax.axis_size("tx")
    tokens, rows = left[0].shape
    wide = right.shape[1]
    tile = 384 if rows % 384 == 0 else rows
    lefts = pl.BlockSpec((tokens, tile), lambda i: (0, i))
    rights = pl.BlockSpec((tokens, wide), lambda i: (0, 0))
    total = pl.pallas_call(
        pair_kernel,
        grid=(rows // tile,),
        in_specs=[lefts, lefts, rights, rights],
        out_specs=pl.BlockSpec((tile, wide), lambda i: (i, 0)),
        out_shape=jax.ShapeDtypeStruct((rows, wide), bf16),
        compiler_params=pltpu.CompilerParams(vmem_limit_bytes=40 * 2**20),
        cost_estimate=pl.CostEstimate(
            flops=4 * tokens * rows * wide, bytes_accessed=2 * rows * wide, transcendentals=0
        ),
    )(*left, right, swap_core(right))
    return total.reshape(chips, -1, wide)


def exchange(blocks):
    return lax.all_to_all(blocks, CHIPS, 0, 0, tiled=True)


def chip_sum(received):
    return jnp.sum(received.astype(f32), axis=0).astype(bf16)


def lineage(segments, parents):
    seg_table = jnp.arange(parents.shape[0], dtype=jnp.int32)
    matches = segments[:, None] == seg_table[None, :]
    parent_seg = jnp.sum(jnp.where(matches, parents[None, :], 0), axis=1)
    matches = parent_seg[:, None] == seg_table[None, :]
    grand_seg = jnp.sum(jnp.where(matches, parents[None, :], 0), axis=1)
    grand_seg = jnp.where(parent_seg >= 0, grand_seg, -1)
    return (parent_seg, grand_seg)


def rope_tables(positions):
    half_size = HD // 2
    frequency = jnp.power(rope_base, -2.0 * jnp.arange(half_size, dtype=f32) / HD)
    angles = positions.astype(f32)[:, None] * frequency[None, :]
    return (jnp.cos(angles), jnp.sin(angles))


def rotate(flat, cosine, sine_table):
    values = flat.reshape(flat.shape[0], -1, HD)
    front = values[..., : HD // 2]
    latter = values[..., HD // 2 :]
    cos_rows = cosine[:, None, :]
    sin_rows = sine_table[:, None, :]
    return jnp.concatenate(
        [front * cos_rows - latter * sin_rows, latter * cos_rows + front * sin_rows], axis=-1
    ).reshape(flat.shape)


def norm_back(upstream, unit_rows, inv_rms):
    return inv_rms * (upstream - unit_rows * jnp.mean(upstream * unit_rows, axis=-1, keepdims=True))


def inverse_rms(rows):
    return lax.rsqrt(jnp.mean(rows * rows, axis=-1, keepdims=True) + norm_eps)


def heads_of(flat):
    return flat.reshape(flat.shape[0], -1, HD)


def side_by_side(left, right):
    count = (right if left is None else left).shape[0]
    parts = [None if t is None else heads_of(t) for t in (left, right)]
    blank = jnp.zeros_like(next(t for t in parts if t is not None))
    parts = [blank if t is None else t for t in parts]
    return jnp.concatenate(parts, axis=2).reshape(count, -1)


def fill_bias(query_ref, key_ref, bias_ref):
    @pl.when(pl.program_id(0) == 0)
    def _():
        seg, parent, grand, index = (query_ref[:, n : n + 1] for n in range(4))

        def fill(n, none):
            key_seg, key_index = key_ref[n, 0:1, :], key_ref[n, 1:2, :]
            allowed = (
                ((key_seg == seg) & (key_index <= index)) | (key_seg == parent) | (key_seg == grand)
            )
            bias_ref[n] = jnp.where(allowed, 0.0, far_below)
            return none

        lax.fori_loop(0, key_ref.shape[0], fill, 0)


def in_token_order(ref, row, chunks):
    height = ref.shape[0] // chunks
    return jnp.concatenate(
        [ref[pl.ds(pl.multiple_of((n ^ row) * height, 16), height), :] for n in range(chunks)], axis=0
    )


def span_of(refs, row, quarter, part, count):
    where = (pl.ds(part * count, count), quarter ^ row)
    return rows_of([ref[where].reshape(-1, 2 * HD) for ref in refs])


def lower(top, change, skip):
    if skip == 0:
        return change(top)
    return jnp.concatenate([top[:skip], change(top[skip:])], axis=0)


def attend_kernel(row_ref, query_ref, key_ref, q_ref, near_ref, far_ref, out_ref, bias_ref):
    chips, chunks, height = near_ref.shape[:3]
    spans = key_ref.shape[0] // chunks
    count = chips // spans
    row = row_ref[0]
    fill_bias(query_ref, key_ref, bias_ref)
    q = in_token_order(q_ref, row, chunks)

    def span(part, carry):
        peak, total, mixed = carry
        keys = [span_of((near_ref, far_ref), row, n, part, count) for n in range(chunks)]
        scores = [
            dot(q[n * height :], keys[n], ((1,), (1,))) + bias_ref[n * spans + part, n * height :, :]
            for n in range(chunks)
        ]
        new_peak = peak
        for n in range(chunks):
            high = jnp.max(scores[n], axis=1, keepdims=True)
            new_peak = lower(new_peak, lambda p: jnp.maximum(p, high), n * height)
        factor = jnp.exp(peak - new_peak)
        total = total * factor
        mixed = mixed * factor
        for n in range(chunks):
            weights = jnp.exp(scores[n] - new_peak[n * height :])
            added = jnp.sum(weights, axis=1, keepdims=True)
            total = lower(total, lambda v: v + added, n * height)
            values = dot(weights.astype(bf16), keys[n])
            mixed = lower(mixed, lambda v: v + values, n * height)
        return new_peak, total, mixed

    start = (
        jnp.full((q.shape[0], 1), far_below, f32),
        jnp.zeros((q.shape[0], 1), f32),
        jnp.zeros((q.shape[0], 2 * HD), f32),
    )
    peak, total, mixed = span(0, start) if spans == 1 else lax.fori_loop(0, spans, span, start)
    lane = lax.broadcasted_iota(jnp.int32, mixed.shape, 1)
    result = jnp.where(lane < HD, peak + jnp.log(total), mixed / total)
    for n in range(chunks):
        out_ref[pl.ds(pl.multiple_of((n ^ row) * height, 16), height), :] = result[
            n * height : (n + 1) * height
        ]


def attend_back_kernel(
    row_ref,
    query_ref,
    key_ref,
    q_ref,
    near_ref,
    far_ref,
    out_ref,
    grad_ref,
    grad_q_ref,
    grad_near_ref,
    grad_far_ref,
    bias_ref,
):
    chips, chunks, height = near_ref.shape[:3]
    spans = key_ref.shape[0] // chunks
    count = chips // spans
    row = row_ref[0]
    fill_bias(query_ref, key_ref, bias_ref)
    q = in_token_order(q_ref, row, chunks)
    grad = in_token_order(grad_ref, row, chunks)
    saved = in_token_order(out_ref, row, chunks)
    log_total = saved[:, 0:1]
    delta = jnp.sum(grad.astype(f32) * saved, axis=1, keepdims=True)

    def span(part, grad_q):
        for n in range(chunks):
            skip = n * height
            keys = span_of((near_ref, far_ref), row, n, part, count)
            scores = dot(q[skip:], keys, ((1,), (1,))) + bias_ref[n * spans + part, skip:, :]
            probs = jnp.exp(scores - log_total[skip:])
            grad_probs = dot(grad[skip:], keys, ((1,), (1,)))
            grad_scores = (probs * (grad_probs - delta[skip:])).astype(bf16)
            added = dot(grad_scores, q[skip:], ((0,), (0,))) + dot(
                probs.astype(bf16), grad[skip:], ((0,), (0,))
            )
            added = added.astype(bf16).reshape(2, count, height, 2 * HD)
            where = (pl.ds(part * count, count), n ^ row)
            grad_near_ref[where] = added[0]
            grad_far_ref[where] = added[1]
            more = dot(grad_scores, keys)
            grad_q = lower(grad_q, lambda v: v + more, skip)
        return grad_q

    start = jnp.zeros((q.shape[0], 2 * HD), f32)
    grad_q = span(0, start) if spans == 1 else lax.fori_loop(0, spans, span, start)
    for n in range(chunks):
        grad_q_ref[pl.ds(pl.multiple_of((n ^ row) * height, 16), height), :] = grad_q[
            n * height : (n + 1) * height
        ]


def attention_specs(queries, kv, query_info, key_info):
    heads = queries.shape[1] // (2 * HD)
    rows = pl.BlockSpec((queries.shape[0], 2 * HD), lambda h: (0, h))
    keys = pl.BlockSpec(kv[0].shape[:3] + (2 * HD,), lambda h: (0, 0, 0, h))
    fixed = [
        pl.BlockSpec(memory_space=pltpu.SMEM),
        pl.BlockSpec(query_info.shape, lambda h: (0, 0)),
        pl.BlockSpec(key_info.shape, lambda h: (0, 0, 0)),
    ]
    bias = pltpu.VMEM((key_info.shape[0], queries.shape[0], key_info.shape[2]), f32)
    params = pltpu.CompilerParams(vmem_limit_bytes=56 * 2**20)
    return heads, rows, keys, fixed, bias, params


def work(kv, products):
    return pl.CostEstimate(
        flops=products * kv[0].size * 16000, bytes_accessed=8 * kv[0].size, transcendentals=0
    )


def attend(row, query_info, key_info, queries, kv):
    heads, rows, keys, fixed, bias, params = attention_specs(queries, kv, query_info, key_info)
    return pl.pallas_call(
        attend_kernel,
        grid=(heads,),
        in_specs=fixed + [rows, keys, keys],
        out_specs=rows,
        out_shape=jax.ShapeDtypeStruct(queries.shape, f32),
        scratch_shapes=[bias],
        compiler_params=params,
        cost_estimate=work(kv, 2),
    )(row, query_info, key_info, queries, *kv)


def attend_back(row, query_info, key_info, queries, kv, saved, grad):
    heads, rows, keys, fixed, bias, params = attention_specs(queries, kv, query_info, key_info)
    return pl.pallas_call(
        attend_back_kernel,
        grid=(heads,),
        in_specs=fixed + [rows, keys, keys, rows, rows],
        out_specs=[rows, keys, keys],
        out_shape=[jax.ShapeDtypeStruct(queries.shape, f32)]
        + [jax.ShapeDtypeStruct(t.shape, bf16) for t in kv],
        scratch_shapes=[bias],
        compiler_params=params,
        cost_estimate=work(kv, 5),
    )(row, query_info, key_info, queries, *kv, saved, grad)


def on_device(
    block_input,
    w_qkv,
    w_out,
    w_gate_up,
    w_down,
    norm_gains,
    cotangent,
    tok_seg,
    tok_pos,
    seg_parent,
):
    rows_n, b_n, x_n, c_n = (lax.axis_size(n) for n in ("za", "pb", "tx", "tc"))
    z, b, x, c = (lax.axis_index(n) for n in ("za", "pb", "tx", "tc"))
    shares = x_n * c_n
    plane = b_n * shares
    own, width = block_input.shape
    piece = width // plane

    def untangle(array, axis, index):
        count = array.shape[axis]
        for bit in range(count.bit_length() - 1):
            step = 1 << bit
            shape = array.shape[:axis] + (count // (2 * step), 2, step) + array.shape[axis + 1 :]
            flipped = jnp.flip(array.reshape(shape), axis + 1).reshape(array.shape)
            array = jnp.where((index >> bit) & 1 == 1, flipped, array)
        return array

    features = w_qkv.shape[2]
    heads = features // HD
    near = (heads + 1) // 2
    units = w_down.shape[0]
    near_units = min(units, (units // 2 + 127) // 128 * 128)
    w_kv = side_by_side(w_qkv[1], w_qkv[2])

    low = 32
    small = jnp.concatenate(
        [norm_gains.reshape(-1)] + [t.astype(bf16) for t in (tok_seg, tok_pos // low, tok_pos % low)]
    )
    small = jnp.pad(small, (0, width - small.shape[0]))[None]
    x_own = block_input
    x_parts = row_send(rows_of([x_own, small]))
    kv_full = plane_gather(*unbundle(turn(bundle([w_kv], [near * 2 * HD])), [2 * features], [near * 2 * HD]))
    q_full = plane_gather(*unbundle(turn(bundle([w_qkv[0]], [near * HD])), [features], [near * HD]))
    first = bundle([w_gate_up[0], w_gate_up[1], w_out.T], [near_units, near_units, near * HD])
    second = bundle([w_down.T], [near_units])
    x_parts, first, second = fence(x_parts, first, second)
    first = turn(first)
    small = rows_of([part[own:] for part in x_parts])
    small = [small] + [
        lax.ppermute(small, "pb", [(i, i ^ k) for i in range(b_n)]) for k in range(1, b_n)
    ]
    small = jnp.stack(small, axis=1)
    gains = small[..., : 2 * norm_gains.shape[1]].reshape(rows_n, b_n, 2, -1)
    group = tok_seg.shape[0]
    small = small[..., gains.shape[3] * 2 :][..., : 3 * group].astype(jnp.int32)
    seg_all = small[..., :group]
    pos_all = small[..., group : 2 * group] * low + small[..., 2 * group :]
    gains = untangle(untangle(gains, 0, z), 1, b).transpose(2, 0, 1, 3).reshape(2, width)
    gains = gains.astype(f32)

    pos_all = untangle(pos_all, 1, b).reshape(rows_n, b_n, x_n, c_n, own)
    seg_all = untangle(untangle(seg_all, 0, z), 1, b).reshape(pos_all.shape)
    index_all = jnp.arange(seg_all.size, dtype=jnp.int32).reshape(seg_all.shape)

    def for_group(array):
        array = lax.dynamic_slice_in_dim(array, b, 1, 1)
        array = lax.dynamic_slice_in_dim(array, x, 1, 2)
        return lax.dynamic_slice_in_dim(array, c, 1, 3).reshape(-1)

    def for_keys(array):
        array = untangle(array, 3, c).transpose(0, 3, 2, 1, 4).reshape(rows_n, 2, -1, 4, own)
        return array.transpose(0, 2, 1, 3, 4).reshape(-1, 8 * own)

    own_seg, own_index, pos_group = for_group(seg_all), for_group(index_all), for_group(pos_all)
    parent_seg, grand_seg = lineage(own_seg, seg_parent)
    query_info = jnp.stack([own_seg, parent_seg, grand_seg, own_index], axis=1)
    key_info = jnp.stack([for_keys(seg_all), for_keys(index_all)], axis=1)
    row = z.astype(jnp.int32).reshape(1)

    cosine, sine_table = rope_tables(pos_group)
    cot_own = cotangent.astype(f32)
    branch_f = (depth_scale * cot_own).astype(bf16)
    rows_a = rows_of([part[:own] for part in x_parts]).astype(f32)
    normed_a = ((rows_a * inverse_rms(rows_a)) * gains[0]).astype(bf16)
    group = rows_n * own
    mine = dot(normed_a, kv_full).reshape(group, heads, 2, HD)
    keys = rotate(mine[:, :, 0].reshape(group, -1), cosine, sine_table).astype(bf16)
    mine = side_by_side(keys, mine[:, :, 1].reshape(group, -1).astype(bf16))
    mine, second, branch_f, query_info, key_info = fence(
        mine, second, branch_f, query_info, key_info
    )
    gate_moved, up_moved, out_moved = unbundle(
        after(first, mine), [units, units, features], [near_units, near_units, near * HD]
    )
    out_full, gate_full, up_full = plane_gather(out_moved), plane_gather(gate_moved), plane_gather(up_moved)
    second = turn(second)
    f_parts = row_send(branch_f)
    chips = b_n * x_n
    kv = exchange(jnp.broadcast_to(mine[None], (chips,) + mine.shape))
    queries = rotate(dot(after(normed_a, mine), q_full), cosine, sine_table)
    queries = side_by_side(queries.astype(bf16) * bf16(HD**-0.5), None)
    kv, second, queries, f_parts = fence(kv, second, queries, f_parts)
    (down_moved,) = unbundle(second, [units], [near_units])
    kv = [t.reshape(chips, rows_n, own, -1) for t in (kv, swap_core(kv))]
    saved = attend(row, query_info, key_info, queries, kv)
    attended = saved.reshape(group, heads, 2, HD)[:, :, 1].reshape(group, -1).astype(bf16)
    mid_part = dot(attended, out_full, ((1,), (1,)))
    parts = row_split(mid_part)
    down_near = exchange(jnp.broadcast_to(down_moved[None], (chips,) + down_moved.shape))
    parts, down_near = fence(parts, down_near)
    down_near = down_near.reshape(-1, units)
    down_full = rows_of([down_near, swap_core(down_near)])
    mid = x_own.astype(f32) + depth_scale * row_sum(parts)
    inv_f = inverse_rms(mid)
    unit_f = mid * inv_f
    normed_f = rows_of(row_send((unit_f * gains[1]).astype(bf16)))
    grad_branch_f = rows_of(f_parts)
    gate = dot(normed_f, gate_full)
    up = dot(normed_f, up_full)
    sig = jax.nn.sigmoid(gate)
    silu = gate * sig
    hidden = (silu * up).astype(bf16)
    gf_twin = with_twin(grad_branch_f)
    nf_twin = with_twin(normed_f)
    grad_hidden = dot(columns(core_halves(grad_branch_f)), down_full)
    grad_gate = (grad_hidden * up * sig * (1.0 + gate * (1.0 - sig))).astype(bf16)
    grad_up = (grad_hidden * silu).astype(bf16)
    normed_part = dot(grad_gate, gate_full, ((1,), (1,))) + dot(grad_up, up_full, ((1,), (1,)))
    down_pair = pair_sum(gf_twin, hidden)
    normed_part, down_pair, hidden, grad_gate, grad_up, nf_twin = fence(
        normed_part, down_pair, hidden, grad_gate, grad_up, nf_twin
    )

    parts = row_split(normed_part)
    down_sum = exchange(down_pair)
    gate_pair = pair_sum(nf_twin, grad_gate)
    up_pair = pair_sum(nf_twin, grad_up)
    parts, down_sum, gate_pair, up_pair = fence(parts, down_sum, gate_pair, up_pair)
    grad_normed_f = row_sum(parts)
    gain_f = jnp.sum(grad_normed_f * unit_f, axis=0)
    grad_mid = cot_own + norm_back(grad_normed_f * gains[1], unit_f, inv_f)
    branch_a = (depth_scale * grad_mid).astype(bf16)

    parts = row_send(branch_a)
    gate_sum = exchange(gate_pair)
    down_sum = chip_sum(down_sum)
    output_part = dot(after(hidden, branch_a), down_full, ((1,), (1,)))
    na_twin = with_twin(after(normed_a, branch_a))
    attended = after(attended, branch_a)
    parts, gate_sum, down_sum, up_pair, output_part, na_twin, attended = fence(
        parts, gate_sum, down_sum, up_pair, output_part, na_twin, attended
    )
    two_back = bundle([down_sum, chip_sum(gate_sum)], [near_units, near_units])
    grad_branch_a = rows_of(parts)
    up_sum = exchange(up_pair)
    output_parts = row_split(output_part)
    grad_attended = dot(grad_branch_a, out_full).astype(bf16)
    grad_q, *grad_kv = attend_back(
        row, query_info, key_info, queries, kv, saved, side_by_side(None, grad_attended)
    )
    grad_q, grad_kv, up_sum, output_parts = fence(grad_q, grad_kv, up_sum, output_parts)

    grad_kv = (grad_kv[0].astype(f32) + swap_core(grad_kv[1]).astype(f32)).astype(bf16)
    grad_kv = grad_kv.reshape(chips, group, -1)
    grad_kv, grad_q, up_sum, two_back, grad_branch_a = fence(
        grad_kv, grad_q, up_sum, two_back, grad_branch_a
    )
    grad_kv = exchange(grad_kv)
    two_back = turn(two_back, True)
    up_back = bundle([chip_sum(up_sum)], [near_units])
    grad_q = grad_q.reshape(group, heads, 2, HD)[:, :, 0].reshape(group, -1) * HD**-0.5
    grad_q = rotate(grad_q, cosine, -sine_table).astype(bf16)
    q_pair = pair_sum(na_twin, grad_q)
    out_pair = pair_sum(with_twin(grad_branch_a), attended)
    two_pair = jnp.concatenate([q_pair, out_pair], axis=2)
    grad_kv, two_pair = fence(grad_kv, two_pair)
    two_sum = exchange(two_pair)
    grad_kv = jnp.sum(grad_kv.astype(f32), axis=0).reshape(group, heads, 2, HD)
    grad_k = rotate(grad_kv[:, :, 0].reshape(group, -1), cosine, -sine_table).astype(bf16)
    grad_kv = side_by_side(grad_k, grad_kv[:, :, 1].reshape(group, -1).astype(bf16))
    normed_part = dot(grad_q, q_full, ((1,), (1,))) + dot(grad_kv, kv_full, ((1,), (1,)))
    grad_kv, normed_part, two_back, up_back = fence(grad_kv, normed_part, two_back, up_back)
    parts = row_split(normed_part)
    kv_pair = pair_sum(na_twin, grad_kv)
    kv_pair, two_sum = fence(kv_pair, two_sum)
    kv_sum = exchange(kv_pair)
    two_sum = chip_sum(two_sum)
    parts, two_sum, up_back = fence(parts, two_sum, up_back)
    up_back = turn(up_back, True)
    grad_normed_a = row_sum(parts)
    output = mid + depth_scale * columns(core_halves(row_sum(output_parts)))
    kv_sum, up_back = fence(kv_sum, up_back)
    last_cuts = [near * 2 * HD, near * HD, near * HD]
    last_back = bundle([chip_sum(kv_sum), two_sum[:, :features], two_sum[:, features:]], last_cuts)
    last_back = turn(last_back, True)

    grad_w_down, grad_w_gate = unbundle(two_back, [units, units], [near_units, near_units])
    (grad_w_up,) = unbundle(up_back, [units], [near_units])
    grad_w_kv, grad_w_q, grad_w_out = unbundle(last_back, [2 * features, features, features], last_cuts)
    grad_gate_up = jnp.stack([grad_w_gate, grad_w_up]).astype(f32)
    grad_down = grad_w_down.astype(f32).T
    grad_out = grad_w_out.astype(f32).T
    grad_w_kv = grad_w_kv.reshape(piece, heads, 2, HD)
    grad_qkv = jnp.stack(
        [grad_w_q] + [grad_w_kv[:, :, n].reshape(piece, features) for n in range(2)]
    ).astype(f32)
    rows_own = x_own.astype(f32)
    inv_a = inverse_rms(rows_own)
    unit_a = rows_own * inv_a
    gain_a = jnp.sum(grad_normed_a * unit_a, axis=0)
    grad_input = grad_mid + norm_back(grad_normed_a * gains[0], unit_a, inv_a)
    gain_sum = jnp.stack([gain_a, gain_f])
    for axis, count in (("tc", c_n), ("tx", x_n), ("pb", b_n), ("za", rows_n)):
        for bit in range(count.bit_length() - 1):
            gain_sum = gain_sum + lax.ppermute(
                gain_sum, axis, [(i, i ^ (1 << bit)) for i in range(count)]
            )
    part = width // (rows_n * plane)
    place = ((z * b_n + b) * x_n + x) * c_n + c
    grad_gains = lax.dynamic_slice_in_dim(gain_sum, place * part, part, 1)
    return (output, grad_input, grad_qkv, grad_out, grad_gate_up, grad_down, grad_gains)


def solution(mesh):
    shares = mesh.shape["tensor"]
    devices = mesh.devices.reshape(shares, -1, shares // 2, 2)
    fine = Mesh(devices, ("za", "pb", "tx", "tc"))
    dp, tensor = ("za", "pb"), ("tx", "tc")
    in_specs = (
        P(dp + tensor, None),
        P(None, dp, tensor),
        P(tensor, dp),
        P(None, dp, tensor),
        P(tensor, dp),
        P(None, dp),
        P(dp + tensor, None),
        P(dp),
        P(dp),
        P(),
    )
    out_specs = (
        P(dp + tensor, None),
        P(dp + tensor, None),
        P(None, dp, tensor),
        P(tensor, dp),
        P(None, dp, tensor),
        P(tensor, dp),
        P(None, dp + tensor),
    )
    return jax.shard_map(
        on_device, mesh=fine, in_specs=in_specs, out_specs=out_specs, check_vma=False
    )
```

```python
import math

import jax
import jax.numpy as jnp
from jax import lax
from jax.experimental import pallas as pl
from jax.experimental.pallas import tpu as pltpu
from jax.sharding import Mesh, PartitionSpec as P

HD = 64

norm_eps = 1e-05
depth_scale = 1.4 / math.sqrt(40.0)
rope_base = 10000.0
far_below = -1e30
f32 = jnp.float32
bf16 = jnp.bfloat16

PLANE = ("tc", "tx", "pb")
CHIPS = ("tx", "pb")
ROW = "za"


def dot(a, b, dims=((1,), (0,))):
    return lax.dot_general(a, b, (dims, ((), ())), preferred_element_type=f32)


def send_row(array, distance):
    return lax.ppermute(array, ROW, [(i, i ^ distance) for i in range(lax.axis_size(ROW))])


def swap_core(array):
    return lax.ppermute(array, "tc", [(0, 1), (1, 0)])


def after(array, *done):
    return lax.optimization_barrier((array,) + done)[0]


def row_send(rows):
    count = lax.axis_size(ROW)
    if count != 4:
        return [rows] + [send_row(rows, k) for k in range(1, count)]
    side, across = send_row(rows, 1), send_row(rows, 2)
    return [rows, side, across, send_row(across, 1)]


def row_split(partial):
    count = lax.axis_size(ROW)
    height = partial.shape[0] // count
    parts = [partial[k * height : (k + 1) * height] for k in range(count)]
    if count != 4:
        return [parts[0]] + [send_row(parts[k].astype(bf16), k) for k in range(1, count)]
    far = send_row(parts[3].astype(bf16), 1)
    return [
        parts[0],
        send_row(parts[1].astype(bf16), 1),
        send_row((parts[2] + far.astype(f32)).astype(bf16), 2),
    ]


def row_sum(parts):
    total = parts[0]
    for part in parts[1:]:
        total = total + part.astype(f32)
    return total


def bundle(arrays, cuts):
    return [
        columns([a[:, :cut] for a, cut in zip(arrays, cuts)]),
        columns([a[:, cut:] for a, cut in zip(arrays, cuts)]),
    ]


def unbundle(parts, widths, cuts):
    arrays, first, second = [], 0, 0
    for wide, cut in zip(widths, cuts):
        rest = wide - cut
        arrays.append(columns([parts[0][:, first : first + cut], parts[1][:, second : second + rest]]))
        first, second = first + cut, second + rest
    return arrays


def turn(parts, back=False):
    rows, shares = lax.axis_size(ROW), lax.axis_size("tx") * lax.axis_size("tc")

    def move(part, twist):
        pairs = [
            (z * shares + t, (t ^ twist) * shares + z % 2 * (shares // 2) + z // 2)
            for z in range(rows)
            for t in range(shares)
        ]
        if back:
            pairs = [(j, i) for i, j in pairs]
        return lax.ppermute(part, (ROW, "tx", "tc"), pairs)

    return [move(parts[0], 0), move(parts[1], shares // 2)]


def columns(parts):
    return jnp.concatenate(parts, axis=1)


def rows_of(parts):
    return jnp.concatenate(parts, axis=0)


def fence(*values):
    return lax.optimization_barrier(values)


def plane_gather(piece):
    return lax.all_gather(piece, PLANE, axis=0, tiled=True)


def core_halves(array):
    half = array.shape[1] // 2
    first = lax.axis_index("tc") == 0
    left, right = array[:, :half], array[:, half:]
    return jnp.where(first, left, right), jnp.where(first, right, left)


def with_twin(left):
    mine, other = core_halves(left)
    return [mine, swap_core(other)]


def pair_kernel(left_ref, left_far_ref, right_ref, right_far_ref, out_ref):
    total = dot(left_ref[...], right_ref[...], ((0,), (0,)))
    total += dot(left_far_ref[...], right_far_ref[...], ((0,), (0,)))
    out_ref[...] = total.astype(bf16)


def pair_sum(left, right):
    chips = lax.axis_size("pb") * lax.axis_size("tx")
    tokens, rows = left[0].shape
    wide = right.shape[1]
    tile = 384 if rows % 384 == 0 else rows
    lefts = pl.BlockSpec((tokens, tile), lambda i: (0, i))
    rights = pl.BlockSpec((tokens, wide), lambda i: (0, 0))
    total = pl.pallas_call(
        pair_kernel,
        grid=(rows // tile,),
        in_specs=[lefts, lefts, rights, rights],
        out_specs=pl.BlockSpec((tile, wide), lambda i: (i, 0)),
        out_shape=jax.ShapeDtypeStruct((rows, wide), bf16),
        compiler_params=pltpu.CompilerParams(vmem_limit_bytes=40 * 2**20),
        cost_estimate=pl.CostEstimate(
            flops=4 * tokens * rows * wide, bytes_accessed=2 * rows * wide, transcendentals=0
        ),
    )(*left, right, swap_core(right))
    return total.reshape(chips, -1, wide)


def near_dot(array, parts):
    half = parts[0].shape[0]
    return dot(array[:, :half], parts[0]) + dot(array[:, half:], parts[1])


def exchange(blocks):
    return lax.all_to_all(blocks, CHIPS, 0, 0, tiled=True)


def chip_sum(received):
    return jnp.sum(received.astype(f32), axis=0).astype(bf16)


def lineage(segments, parents):
    seg_table = jnp.arange(parents.shape[0], dtype=jnp.int32)
    matches = segments[:, None] == seg_table[None, :]
    parent_seg = jnp.sum(jnp.where(matches, parents[None, :], 0), axis=1)
    matches = parent_seg[:, None] == seg_table[None, :]
    grand_seg = jnp.sum(jnp.where(matches, parents[None, :], 0), axis=1)
    grand_seg = jnp.where(parent_seg >= 0, grand_seg, -1)
    return (parent_seg, grand_seg)


def rope_tables(positions):
    half_size = HD // 2
    frequency = jnp.power(rope_base, -2.0 * jnp.arange(half_size, dtype=f32) / HD)
    angles = positions.astype(f32)[:, None] * frequency[None, :]
    return (jnp.cos(angles), jnp.sin(angles))


def rotate(flat, cosine, sine_table):
    values = flat.reshape(flat.shape[0], -1, HD)
    front = values[..., : HD // 2]
    latter = values[..., HD // 2 :]
    cos_rows = cosine[:, None, :]
    sin_rows = sine_table[:, None, :]
    return jnp.concatenate(
        [front * cos_rows - latter * sin_rows, latter * cos_rows + front * sin_rows], axis=-1
    ).reshape(flat.shape)


def norm_back(upstream, unit_rows, inv_rms):
    return inv_rms * (upstream - unit_rows * jnp.mean(upstream * unit_rows, axis=-1, keepdims=True))


def inverse_rms(rows):
    return lax.rsqrt(jnp.mean(rows * rows, axis=-1, keepdims=True) + norm_eps)


def heads_of(flat):
    return flat.reshape(flat.shape[0], -1, HD)


def side_by_side(left, right):
    count = (right if left is None else left).shape[0]
    parts = [None if t is None else heads_of(t) for t in (left, right)]
    blank = jnp.zeros_like(next(t for t in parts if t is not None))
    parts = [blank if t is None else t for t in parts]
    return jnp.concatenate(parts, axis=2).reshape(count, -1)


def fill_bias(query_ref, key_ref, bias_ref):
    @pl.when(pl.program_id(0) == 0)
    def _():
        seg, parent, grand, index = (query_ref[:, n : n + 1] for n in range(4))

        def fill(n, none):
            key_seg, key_index = key_ref[n, 0:1, :], key_ref[n, 1:2, :]
            allowed = (
                ((key_seg == seg) & (key_index <= index)) | (key_seg == parent) | (key_seg == grand)
            )
            bias_ref[n] = jnp.where(allowed, 0.0, far_below)
            return none

        lax.fori_loop(0, key_ref.shape[0], fill, 0)


def in_token_order(ref, row, chunks):
    height = ref.shape[0] // chunks
    return jnp.concatenate(
        [ref[pl.ds(pl.multiple_of((n ^ row) * height, 16), height), :] for n in range(chunks)], axis=0
    )


def span_of(refs, row, quarter, part, count):
    where = (pl.ds(part * count, count), quarter ^ row)
    return rows_of([ref[where].reshape(-1, 2 * HD) for ref in refs])


def lower(top, change, skip):
    if skip == 0:
        return change(top)
    return jnp.concatenate([top[:skip], change(top[skip:])], axis=0)


def attend_kernel(row_ref, query_ref, key_ref, q_ref, near_ref, far_ref, out_ref, bias_ref):
    chips, chunks, height = near_ref.shape[:3]
    spans = key_ref.shape[0] // chunks
    count = chips // spans
    row = row_ref[0]
    fill_bias(query_ref, key_ref, bias_ref)
    q = in_token_order(q_ref, row, chunks)

    def span(part, carry):
        peak, total, mixed = carry
        keys = [span_of((near_ref, far_ref), row, n, part, count) for n in range(chunks)]
        scores = [
            dot(q[n * height :], keys[n], ((1,), (1,))) + bias_ref[n * spans + part, n * height :, :]
            for n in range(chunks)
        ]
        new_peak = peak
        for n in range(chunks):
            high = jnp.max(scores[n], axis=1, keepdims=True)
            new_peak = lower(new_peak, lambda p: jnp.maximum(p, high), n * height)
        factor = jnp.exp(peak - new_peak)
        total = total * factor
        mixed = mixed * factor
        for n in range(chunks):
            weights = jnp.exp(scores[n] - new_peak[n * height :])
            added = jnp.sum(weights, axis=1, keepdims=True)
            total = lower(total, lambda v: v + added, n * height)
            values = dot(weights.astype(bf16), keys[n])
            mixed = lower(mixed, lambda v: v + values, n * height)
        return new_peak, total, mixed

    start = (
        jnp.full((q.shape[0], 1), far_below, f32),
        jnp.zeros((q.shape[0], 1), f32),
        jnp.zeros((q.shape[0], 2 * HD), f32),
    )
    peak, total, mixed = span(0, start) if spans == 1 else lax.fori_loop(0, spans, span, start)
    lane = lax.broadcasted_iota(jnp.int32, mixed.shape, 1)
    result = jnp.where(lane < HD, peak + jnp.log(total), mixed / total)
    for n in range(chunks):
        out_ref[pl.ds(pl.multiple_of((n ^ row) * height, 16), height), :] = result[
            n * height : (n + 1) * height
        ]


def attend_back_kernel(
    row_ref,
    query_ref,
    key_ref,
    q_ref,
    near_ref,
    far_ref,
    out_ref,
    grad_ref,
    grad_q_ref,
    grad_near_ref,
    grad_far_ref,
    bias_ref,
):
    chips, chunks, height = near_ref.shape[:3]
    spans = key_ref.shape[0] // chunks
    count = chips // spans
    row = row_ref[0]
    fill_bias(query_ref, key_ref, bias_ref)
    q = in_token_order(q_ref, row, chunks)
    grad = in_token_order(grad_ref, row, chunks)
    saved = in_token_order(out_ref, row, chunks)
    log_total = saved[:, 0:1]
    delta = jnp.sum(grad.astype(f32) * saved, axis=1, keepdims=True)

    def span(part, grad_q):
        for n in range(chunks):
            skip = n * height
            keys = span_of((near_ref, far_ref), row, n, part, count)
            scores = dot(q[skip:], keys, ((1,), (1,))) + bias_ref[n * spans + part, skip:, :]
            probs = jnp.exp(scores - log_total[skip:])
            grad_probs = dot(grad[skip:], keys, ((1,), (1,)))
            grad_scores = (probs * (grad_probs - delta[skip:])).astype(bf16)
            added = dot(grad_scores, q[skip:], ((0,), (0,))) + dot(
                probs.astype(bf16), grad[skip:], ((0,), (0,))
            )
            added = added.astype(bf16).reshape(2, count, height, 2 * HD)
            where = (pl.ds(part * count, count), n ^ row)
            grad_near_ref[where] = added[0]
            grad_far_ref[where] = added[1]
            more = dot(grad_scores, keys)
            grad_q = lower(grad_q, lambda v: v + more, skip)
        return grad_q

    start = jnp.zeros((q.shape[0], 2 * HD), f32)
    grad_q = span(0, start) if spans == 1 else lax.fori_loop(0, spans, span, start)
    for n in range(chunks):
        grad_q_ref[pl.ds(pl.multiple_of((n ^ row) * height, 16), height), :] = grad_q[
            n * height : (n + 1) * height
        ]


def attention_specs(queries, kv, query_info, key_info):
    heads = queries.shape[1] // (2 * HD)
    rows = pl.BlockSpec((queries.shape[0], 2 * HD), lambda h: (0, h))
    keys = pl.BlockSpec(kv[0].shape[:3] + (2 * HD,), lambda h: (0, 0, 0, h))
    fixed = [
        pl.BlockSpec(memory_space=pltpu.SMEM),
        pl.BlockSpec(query_info.shape, lambda h: (0, 0)),
        pl.BlockSpec(key_info.shape, lambda h: (0, 0, 0)),
    ]
    bias = pltpu.VMEM((key_info.shape[0], queries.shape[0], key_info.shape[2]), f32)
    params = pltpu.CompilerParams(vmem_limit_bytes=56 * 2**20)
    return heads, rows, keys, fixed, bias, params


def work(kv, products):
    return pl.CostEstimate(
        flops=products * kv[0].size * 16000, bytes_accessed=8 * kv[0].size, transcendentals=0
    )


def attend(row, query_info, key_info, queries, kv):
    heads, rows, keys, fixed, bias, params = attention_specs(queries, kv, query_info, key_info)
    return pl.pallas_call(
        attend_kernel,
        grid=(heads,),
        in_specs=fixed + [rows, keys, keys],
        out_specs=rows,
        out_shape=jax.ShapeDtypeStruct(queries.shape, f32),
        scratch_shapes=[bias],
        compiler_params=params,
        cost_estimate=work(kv, 2),
    )(row, query_info, key_info, queries, *kv)


def attend_back(row, query_info, key_info, queries, kv, saved, grad):
    heads, rows, keys, fixed, bias, params = attention_specs(queries, kv, query_info, key_info)
    return pl.pallas_call(
        attend_back_kernel,
        grid=(heads,),
        in_specs=fixed + [rows, keys, keys, rows, rows],
        out_specs=[rows, keys, keys],
        out_shape=[jax.ShapeDtypeStruct(queries.shape, f32)]
        + [jax.ShapeDtypeStruct(t.shape, bf16) for t in kv],
        scratch_shapes=[bias],
        compiler_params=params,
        cost_estimate=work(kv, 5),
    )(row, query_info, key_info, queries, *kv, saved, grad)


def on_device(
    block_input,
    w_qkv,
    w_out,
    w_gate_up,
    w_down,
    norm_gains,
    cotangent,
    tok_seg,
    tok_pos,
    seg_parent,
):
    rows_n, b_n, x_n, c_n = (lax.axis_size(n) for n in ("za", "pb", "tx", "tc"))
    z, b, x, c = (lax.axis_index(n) for n in ("za", "pb", "tx", "tc"))
    shares = x_n * c_n
    plane = b_n * shares
    own, width = block_input.shape
    piece = width // plane

    def untangle(array, axis, index):
        count = array.shape[axis]
        for bit in range(count.bit_length() - 1):
            step = 1 << bit
            shape = array.shape[:axis] + (count // (2 * step), 2, step) + array.shape[axis + 1 :]
            flipped = jnp.flip(array.reshape(shape), axis + 1).reshape(array.shape)
            array = jnp.where((index >> bit) & 1 == 1, flipped, array)
        return array

    features = w_qkv.shape[2]
    heads = features // HD
    near = (heads + 1) // 2
    units = w_down.shape[0]
    near_units = min(units, (units // 2 + 127) // 128 * 128)
    w_kv = side_by_side(w_qkv[1], w_qkv[2])

    low = 32
    small = jnp.concatenate(
        [norm_gains.reshape(-1)] + [t.astype(bf16) for t in (tok_seg, tok_pos // low, tok_pos % low)]
    )
    small = jnp.pad(small, (0, width - small.shape[0]))[None]
    x_own = block_input
    x_parts = row_send(rows_of([x_own, small]))
    kv_full = plane_gather(*unbundle(turn(bundle([w_kv], [near * 2 * HD])), [2 * features], [near * 2 * HD]))
    q_full = plane_gather(*unbundle(turn(bundle([w_qkv[0]], [near * HD])), [features], [near * HD]))
    first = bundle([w_gate_up[0], w_out.T], [near_units, near * HD])
    second = bundle([w_gate_up[1], w_down.T], [near_units, near_units])
    x_parts, first, second = fence(x_parts, first, second)
    first = turn(first)
    small = rows_of([part[own:] for part in x_parts])
    small = [small] + [
        lax.ppermute(small, "pb", [(i, i ^ k) for i in range(b_n)]) for k in range(1, b_n)
    ]
    small = jnp.stack(small, axis=1)
    gains = small[..., : 2 * norm_gains.shape[1]].reshape(rows_n, b_n, 2, -1)
    group = tok_seg.shape[0]
    small = small[..., gains.shape[3] * 2 :][..., : 3 * group].astype(jnp.int32)
    seg_all = small[..., :group]
    pos_all = small[..., group : 2 * group] * low + small[..., 2 * group :]
    gains = untangle(untangle(gains, 0, z), 1, b).transpose(2, 0, 1, 3).reshape(2, width)
    gains = gains.astype(f32)

    pos_all = untangle(pos_all, 1, b).reshape(rows_n, b_n, x_n, c_n, own)
    seg_all = untangle(untangle(seg_all, 0, z), 1, b).reshape(pos_all.shape)
    index_all = jnp.arange(seg_all.size, dtype=jnp.int32).reshape(seg_all.shape)

    def for_group(array):
        array = lax.dynamic_slice_in_dim(array, b, 1, 1)
        array = lax.dynamic_slice_in_dim(array, x, 1, 2)
        return lax.dynamic_slice_in_dim(array, c, 1, 3).reshape(-1)

    def for_keys(array):
        array = untangle(array, 3, c).transpose(0, 3, 2, 1, 4).reshape(rows_n, 2, -1, 4, own)
        return array.transpose(0, 2, 1, 3, 4).reshape(-1, 8 * own)

    own_seg, own_index, pos_group = for_group(seg_all), for_group(index_all), for_group(pos_all)
    parent_seg, grand_seg = lineage(own_seg, seg_parent)
    query_info = jnp.stack([own_seg, parent_seg, grand_seg, own_index], axis=1)
    key_info = jnp.stack([for_keys(seg_all), for_keys(index_all)], axis=1)
    row = z.astype(jnp.int32).reshape(1)

    cosine, sine_table = rope_tables(pos_group)
    cot_own = cotangent.astype(f32)
    branch_f = (depth_scale * cot_own).astype(bf16)
    rows_a = rows_of([part[:own] for part in x_parts]).astype(f32)
    normed_a = ((rows_a * inverse_rms(rows_a)) * gains[0]).astype(bf16)
    group = rows_n * own
    mine = dot(normed_a, kv_full).reshape(group, heads, 2, HD)
    keys = rotate(mine[:, :, 0].reshape(group, -1), cosine, sine_table).astype(bf16)
    mine = side_by_side(keys, mine[:, :, 1].reshape(group, -1).astype(bf16))
    mine, second, branch_f, query_info, key_info = fence(
        mine, second, branch_f, query_info, key_info
    )
    gate_moved, out_moved = unbundle(after(first, mine), [units, features], [near_units, near * HD])
    out_full, gate_full = plane_gather(out_moved), plane_gather(gate_moved)
    second = turn(second)
    f_parts = row_send(branch_f)
    chips = b_n * x_n
    kv = exchange(jnp.broadcast_to(mine[None], (chips,) + mine.shape))
    queries = rotate(dot(after(normed_a, mine), q_full), cosine, sine_table)
    queries = side_by_side(queries.astype(bf16) * bf16(HD**-0.5), None)
    kv, second, queries, f_parts = fence(kv, second, queries, f_parts)
    up_moved, down_moved = unbundle(second, [units, units], [near_units, near_units])
    up_full = plane_gather(up_moved)
    kv = [t.reshape(chips, rows_n, own, -1) for t in (kv, swap_core(kv))]
    saved = attend(row, query_info, key_info, queries, kv)
    attended = saved.reshape(group, heads, 2, HD)[:, :, 1].reshape(group, -1).astype(bf16)
    mid_part = dot(attended, out_full, ((1,), (1,)))
    parts = row_split(mid_part)
    down_near = exchange(jnp.broadcast_to(down_moved[None], (chips,) + down_moved.shape))
    parts, down_near = fence(parts, down_near)
    down_near = down_near.reshape(-1, units)
    down_full = [down_near, swap_core(down_near)]
    mid = x_own.astype(f32) + depth_scale * row_sum(parts)
    inv_f = inverse_rms(mid)
    unit_f = mid * inv_f
    normed_f = rows_of(row_send((unit_f * gains[1]).astype(bf16)))
    grad_branch_f = rows_of(f_parts)
    gate = dot(normed_f, gate_full)
    up = dot(normed_f, up_full)
    sig = jax.nn.sigmoid(gate)
    silu = gate * sig
    hidden = (silu * up).astype(bf16)
    gf_twin = with_twin(grad_branch_f)
    nf_twin = with_twin(normed_f)
    grad_hidden = near_dot(columns(core_halves(grad_branch_f)), down_full)
    grad_gate = (grad_hidden * up * sig * (1.0 + gate * (1.0 - sig))).astype(bf16)
    grad_up = (grad_hidden * silu).astype(bf16)
    normed_part = dot(grad_gate, gate_full, ((1,), (1,))) + dot(grad_up, up_full, ((1,), (1,)))
    down_pair = pair_sum(gf_twin, hidden)
    normed_part, down_pair, hidden, grad_gate, grad_up, nf_twin = fence(
        normed_part, down_pair, hidden, grad_gate, grad_up, nf_twin
    )

    parts = row_split(normed_part)
    down_sum = exchange(down_pair)
    gate_pair = pair_sum(nf_twin, grad_gate)
    up_pair = pair_sum(nf_twin, grad_up)
    parts, down_sum, gate_pair, up_pair = fence(parts, down_sum, gate_pair, up_pair)
    grad_normed_f = row_sum(parts)
    gain_f = jnp.sum(grad_normed_f * unit_f, axis=0)
    grad_mid = cot_own + norm_back(grad_normed_f * gains[1], unit_f, inv_f)
    branch_a = (depth_scale * grad_mid).astype(bf16)

    parts = row_send(branch_a)
    gate_sum = exchange(gate_pair)
    down_sum = chip_sum(down_sum)
    output_part = columns([dot(after(hidden, branch_a), t, ((1,), (1,))) for t in down_full])
    na_twin = with_twin(after(normed_a, branch_a))
    attended = after(attended, branch_a)
    parts, gate_sum, down_sum, up_pair, output_part, na_twin, attended = fence(
        parts, gate_sum, down_sum, up_pair, output_part, na_twin, attended
    )
    two_back = bundle([down_sum, chip_sum(gate_sum)], [near_units, near_units])
    grad_branch_a = rows_of(parts)
    up_sum = exchange(up_pair)
    output_parts = row_split(output_part)
    grad_attended = dot(grad_branch_a, out_full).astype(bf16)
    grad_q, *grad_kv = attend_back(
        row, query_info, key_info, queries, kv, saved, side_by_side(None, grad_attended)
    )
    grad_q, grad_kv, up_sum, output_parts = fence(grad_q, grad_kv, up_sum, output_parts)

    grad_kv = (grad_kv[0].astype(f32) + swap_core(grad_kv[1]).astype(f32)).astype(bf16)
    grad_kv = grad_kv.reshape(chips, group, -1)
    grad_kv, grad_q, up_sum, two_back, grad_branch_a = fence(
        grad_kv, grad_q, up_sum, two_back, grad_branch_a
    )
    grad_kv = exchange(grad_kv)
    two_back = turn(two_back, True)
    up_back = bundle([chip_sum(up_sum)], [near_units])
    grad_q = grad_q.reshape(group, heads, 2, HD)[:, :, 0].reshape(group, -1) * HD**-0.5
    grad_q = rotate(grad_q, cosine, -sine_table).astype(bf16)
    q_pair = pair_sum(na_twin, grad_q)
    out_pair = pair_sum(with_twin(grad_branch_a), attended)
    two_pair = jnp.concatenate([q_pair, out_pair], axis=2)
    grad_kv, two_pair = fence(grad_kv, two_pair)
    two_sum = exchange(two_pair)
    grad_kv = jnp.sum(grad_kv.astype(f32), axis=0).reshape(group, heads, 2, HD)
    grad_k = rotate(grad_kv[:, :, 0].reshape(group, -1), cosine, -sine_table).astype(bf16)
    grad_kv = side_by_side(grad_k, grad_kv[:, :, 1].reshape(group, -1).astype(bf16))
    normed_part = dot(grad_q, q_full, ((1,), (1,))) + dot(grad_kv, kv_full, ((1,), (1,)))
    grad_kv, normed_part, two_back, up_back = fence(grad_kv, normed_part, two_back, up_back)
    parts = row_split(normed_part)
    kv_pair = pair_sum(na_twin, grad_kv)
    kv_pair, two_sum = fence(kv_pair, two_sum)
    kv_sum = exchange(kv_pair)
    two_sum = chip_sum(two_sum)
    parts, two_sum, up_back = fence(parts, two_sum, up_back)
    up_back = turn(up_back, True)
    grad_normed_a = row_sum(parts)
    output = mid + depth_scale * columns(core_halves(row_sum(output_parts)))
    kv_sum, up_back = fence(kv_sum, up_back)
    last_cuts = [near * 2 * HD, near * HD, near * HD]
    last_back = bundle([chip_sum(kv_sum), two_sum[:, :features], two_sum[:, features:]], last_cuts)
    last_back = turn(last_back, True)

    grad_w_down, grad_w_gate = unbundle(two_back, [units, units], [near_units, near_units])
    (grad_w_up,) = unbundle(up_back, [units], [near_units])
    grad_w_kv, grad_w_q, grad_w_out = unbundle(last_back, [2 * features, features, features], last_cuts)
    grad_gate_up = jnp.stack([grad_w_gate, grad_w_up]).astype(f32)
    grad_down = grad_w_down.astype(f32).T
    grad_out = grad_w_out.astype(f32).T
    grad_w_kv = grad_w_kv.reshape(piece, heads, 2, HD)
    grad_qkv = jnp.stack(
        [grad_w_q] + [grad_w_kv[:, :, n].reshape(piece, features) for n in range(2)]
    ).astype(f32)
    rows_own = x_own.astype(f32)
    inv_a = inverse_rms(rows_own)
    unit_a = rows_own * inv_a
    gain_a = jnp.sum(grad_normed_a * unit_a, axis=0)
    grad_input = grad_mid + norm_back(grad_normed_a * gains[0], unit_a, inv_a)
    gain_sum = jnp.stack([gain_a, gain_f])
    for axis, count in (("tc", c_n), ("tx", x_n), ("pb", b_n), ("za", rows_n)):
        for bit in range(count.bit_length() - 1):
            gain_sum = gain_sum + lax.ppermute(
                gain_sum, axis, [(i, i ^ (1 << bit)) for i in range(count)]
            )
    part = width // (rows_n * plane)
    place = ((z * b_n + b) * x_n + x) * c_n + c
    grad_gains = lax.dynamic_slice_in_dim(gain_sum, place * part, part, 1)
    return (output, grad_input, grad_qkv, grad_out, grad_gate_up, grad_down, grad_gains)


def solution(mesh):
    shares = mesh.shape["tensor"]
    devices = mesh.devices.reshape(shares, -1, shares // 2, 2)
    fine = Mesh(devices, ("za", "pb", "tx", "tc"))
    dp, tensor = ("za", "pb"), ("tx", "tc")
    in_specs = (
        P(dp + tensor, None),
        P(None, dp, tensor),
        P(tensor, dp),
        P(None, dp, tensor),
        P(tensor, dp),
        P(None, dp),
        P(dp + tensor, None),
        P(dp),
        P(dp),
        P(),
    )
    out_specs = (
        P(dp + tensor, None),
        P(dp + tensor, None),
        P(None, dp, tensor),
        P(tensor, dp),
        P(None, dp, tensor),
        P(tensor, dp),
        P(None, dp + tensor),
    )
    return jax.shard_map(
        on_device, mesh=fine, in_specs=in_specs, out_specs=out_specs, check_vma=False
    )
```

```python
import math

import jax
import jax.numpy as jnp
from jax import lax
from jax.experimental import pallas as pl
from jax.experimental.pallas import tpu as pltpu
from jax.sharding import Mesh, PartitionSpec as P

HD = 64

norm_eps = 1e-05
depth_scale = 1.4 / math.sqrt(40.0)
rope_base = 10000.0
far_below = -1e30
f32 = jnp.float32
bf16 = jnp.bfloat16

PLANE = ("tc", "tx", "pb")
CHIPS = ("tx", "pb")
ROW = "za"


def dot(a, b, dims=((1,), (0,))):
    return lax.dot_general(a, b, (dims, ((), ())), preferred_element_type=f32)


def send_row(array, distance):
    return lax.ppermute(array, ROW, [(i, i ^ distance) for i in range(lax.axis_size(ROW))])


def swap_core(array):
    return lax.ppermute(array, "tc", [(0, 1), (1, 0)])


def after(array, *done):
    return lax.optimization_barrier((array,) + done)[0]


def row_send(rows):
    count = lax.axis_size(ROW)
    if count != 4:
        return [rows] + [send_row(rows, k) for k in range(1, count)]
    side, across = send_row(rows, 1), send_row(rows, 2)
    return [rows, side, across, send_row(across, 1)]


def row_split(partial):
    count = lax.axis_size(ROW)
    height = partial.shape[0] // count
    parts = [partial[k * height : (k + 1) * height] for k in range(count)]
    if count != 4:
        return [parts[0]] + [send_row(parts[k].astype(bf16), k) for k in range(1, count)]
    far = send_row(parts[3].astype(bf16), 1)
    return [
        parts[0],
        send_row(parts[1].astype(bf16), 1),
        send_row((parts[2] + far.astype(f32)).astype(bf16), 2),
    ]


def row_sum(parts):
    total = parts[0]
    for part in parts[1:]:
        total = total + part.astype(f32)
    return total


def bundle(arrays, cuts):
    return [
        columns([a[:, :cut] for a, cut in zip(arrays, cuts)]),
        columns([a[:, cut:] for a, cut in zip(arrays, cuts)]),
    ]


def unbundle(parts, widths, cuts):
    arrays, first, second = [], 0, 0
    for wide, cut in zip(widths, cuts):
        rest = wide - cut
        arrays.append(columns([parts[0][:, first : first + cut], parts[1][:, second : second + rest]]))
        first, second = first + cut, second + rest
    return arrays


def turn(parts, back=False):
    rows, shares = lax.axis_size(ROW), lax.axis_size("tx") * lax.axis_size("tc")

    def move(part, twist):
        pairs = [
            (z * shares + t, (t ^ twist) * shares + z % 2 * (shares // 2) + z // 2)
            for z in range(rows)
            for t in range(shares)
        ]
        if back:
            pairs = [(j, i) for i, j in pairs]
        return lax.ppermute(part, (ROW, "tx", "tc"), pairs)

    return [move(parts[0], 0), move(parts[1], shares // 2)]


def columns(parts):
    return jnp.concatenate(parts, axis=1)


def rows_of(parts):
    return jnp.concatenate(parts, axis=0)


def fence(*values):
    return lax.optimization_barrier(values)


def plane_gather(piece):
    return lax.all_gather(piece, PLANE, axis=0, tiled=True)


def core_halves(array):
    half = array.shape[1] // 2
    first = lax.axis_index("tc") == 0
    left, right = array[:, :half], array[:, half:]
    return jnp.where(first, left, right), jnp.where(first, right, left)


def with_twin(left):
    mine, other = core_halves(left)
    return [mine, swap_core(other)]


def pair_kernel(left_ref, left_far_ref, right_ref, right_far_ref, out_ref):
    total = dot(left_ref[...], right_ref[...], ((0,), (0,)))
    total += dot(left_far_ref[...], right_far_ref[...], ((0,), (0,)))
    out_ref[...] = total.astype(bf16)


def pair_sum(left, right):
    chips = lax.axis_size("pb") * lax.axis_size("tx")
    tokens, rows = left[0].shape
    wide = right.shape[1]
    tile = 128 if rows % 128 == 0 else rows
    lefts = pl.BlockSpec((tokens, tile), lambda i: (0, i))
    rights = pl.BlockSpec((tokens, wide), lambda i: (0, 0))
    total = pl.pallas_call(
        pair_kernel,
        grid=(rows // tile,),
        in_specs=[lefts, lefts, rights, rights],
        out_specs=pl.BlockSpec((tile, wide), lambda i: (i, 0)),
        out_shape=jax.ShapeDtypeStruct((rows, wide), bf16),
        compiler_params=pltpu.CompilerParams(vmem_limit_bytes=40 * 2**20),
        cost_estimate=pl.CostEstimate(
            flops=4 * tokens * rows * wide, bytes_accessed=2 * rows * wide, transcendentals=0
        ),
    )(*left, right, swap_core(right))
    return total.reshape(chips, -1, wide)


def near_dot(array, parts):
    half = parts[0].shape[0]
    return dot(array[:, :half], parts[0]) + dot(array[:, half:], parts[1])


def exchange(blocks):
    return lax.all_to_all(blocks, CHIPS, 0, 0, tiled=True)


def chip_sum(received):
    return jnp.sum(received.astype(f32), axis=0).astype(bf16)


def lineage(segments, parents):
    seg_table = jnp.arange(parents.shape[0], dtype=jnp.int32)
    matches = segments[:, None] == seg_table[None, :]
    parent_seg = jnp.sum(jnp.where(matches, parents[None, :], 0), axis=1)
    matches = parent_seg[:, None] == seg_table[None, :]
    grand_seg = jnp.sum(jnp.where(matches, parents[None, :], 0), axis=1)
    grand_seg = jnp.where(parent_seg >= 0, grand_seg, -1)
    return (parent_seg, grand_seg)


def rope_tables(positions):
    half_size = HD // 2
    frequency = jnp.power(rope_base, -2.0 * jnp.arange(half_size, dtype=f32) / HD)
    angles = positions.astype(f32)[:, None] * frequency[None, :]
    return (jnp.cos(angles), jnp.sin(angles))


def rotate(flat, cosine, sine_table):
    values = flat.reshape(flat.shape[0], -1, HD)
    front = values[..., : HD // 2]
    latter = values[..., HD // 2 :]
    cos_rows = cosine[:, None, :]
    sin_rows = sine_table[:, None, :]
    return jnp.concatenate(
        [front * cos_rows - latter * sin_rows, latter * cos_rows + front * sin_rows], axis=-1
    ).reshape(flat.shape)


def norm_back(upstream, unit_rows, inv_rms):
    return inv_rms * (upstream - unit_rows * jnp.mean(upstream * unit_rows, axis=-1, keepdims=True))


def inverse_rms(rows):
    return lax.rsqrt(jnp.mean(rows * rows, axis=-1, keepdims=True) + norm_eps)


def heads_of(flat):
    return flat.reshape(flat.shape[0], -1, HD)


def side_by_side(left, right):
    count = (right if left is None else left).shape[0]
    parts = [None if t is None else heads_of(t) for t in (left, right)]
    blank = jnp.zeros_like(next(t for t in parts if t is not None))
    parts = [blank if t is None else t for t in parts]
    return jnp.concatenate(parts, axis=2).reshape(count, -1)


def fill_bias(query_ref, key_ref, bias_ref):
    @pl.when(pl.program_id(0) == 0)
    def _():
        seg, parent, grand, index = (query_ref[:, n : n + 1] for n in range(4))

        def fill(n, none):
            key_seg, key_index = key_ref[n, 0:1, :], key_ref[n, 1:2, :]
            allowed = (
                ((key_seg == seg) & (key_index <= index)) | (key_seg == parent) | (key_seg == grand)
            )
            bias_ref[n] = jnp.where(allowed, 0.0, far_below)
            return none

        lax.fori_loop(0, key_ref.shape[0], fill, 0)


def in_token_order(ref, row, chunks):
    height = ref.shape[0] // chunks
    return jnp.concatenate(
        [ref[pl.ds(pl.multiple_of((n ^ row) * height, 16), height), :] for n in range(chunks)], axis=0
    )


def span_of(refs, row, quarter, part, count):
    where = (pl.ds(part * count, count), quarter ^ row)
    return rows_of([ref[where].reshape(-1, 2 * HD) for ref in refs])


def lower(top, change, skip):
    if skip == 0:
        return change(top)
    return jnp.concatenate([top[:skip], change(top[skip:])], axis=0)


def attend_kernel(row_ref, query_ref, key_ref, q_ref, near_ref, far_ref, out_ref, bias_ref):
    chips, chunks, height = near_ref.shape[:3]
    spans = key_ref.shape[0] // chunks
    count = chips // spans
    row = row_ref[0]
    fill_bias(query_ref, key_ref, bias_ref)
    q = in_token_order(q_ref, row, chunks)

    def span(part, carry):
        peak, total, mixed = carry
        keys = [span_of((near_ref, far_ref), row, n, part, count) for n in range(chunks)]
        scores = [
            dot(q[n * height :], keys[n], ((1,), (1,))) + bias_ref[n * spans + part, n * height :, :]
            for n in range(chunks)
        ]
        new_peak = peak
        for n in range(chunks):
            high = jnp.max(scores[n], axis=1, keepdims=True)
            new_peak = lower(new_peak, lambda p: jnp.maximum(p, high), n * height)
        factor = jnp.exp(peak - new_peak)
        total = total * factor
        mixed = mixed * factor
        for n in range(chunks):
            weights = jnp.exp(scores[n] - new_peak[n * height :])
            added = jnp.sum(weights, axis=1, keepdims=True)
            total = lower(total, lambda v: v + added, n * height)
            values = dot(weights.astype(bf16), keys[n])
            mixed = lower(mixed, lambda v: v + values, n * height)
        return new_peak, total, mixed

    start = (
        jnp.full((q.shape[0], 1), far_below, f32),
        jnp.zeros((q.shape[0], 1), f32),
        jnp.zeros((q.shape[0], 2 * HD), f32),
    )
    peak, total, mixed = span(0, start) if spans == 1 else lax.fori_loop(0, spans, span, start)
    lane = lax.broadcasted_iota(jnp.int32, mixed.shape, 1)
    result = jnp.where(lane < HD, peak + jnp.log(total), mixed / total)
    for n in range(chunks):
        out_ref[pl.ds(pl.multiple_of((n ^ row) * height, 16), height), :] = result[
            n * height : (n + 1) * height
        ]


def attend_back_kernel(
    row_ref,
    query_ref,
    key_ref,
    q_ref,
    near_ref,
    far_ref,
    out_ref,
    grad_ref,
    grad_q_ref,
    grad_near_ref,
    grad_far_ref,
    bias_ref,
):
    chips, chunks, height = near_ref.shape[:3]
    spans = key_ref.shape[0] // chunks
    count = chips // spans
    row = row_ref[0]
    fill_bias(query_ref, key_ref, bias_ref)
    q = in_token_order(q_ref, row, chunks)
    grad = in_token_order(grad_ref, row, chunks)
    saved = in_token_order(out_ref, row, chunks)
    log_total = saved[:, 0:1]
    delta = jnp.sum(grad.astype(f32) * saved, axis=1, keepdims=True)

    def span(part, grad_q):
        for n in range(chunks):
            skip = n * height
            keys = span_of((near_ref, far_ref), row, n, part, count)
            scores = dot(q[skip:], keys, ((1,), (1,))) + bias_ref[n * spans + part, skip:, :]
            probs = jnp.exp(scores - log_total[skip:])
            grad_probs = dot(grad[skip:], keys, ((1,), (1,)))
            grad_scores = (probs * (grad_probs - delta[skip:])).astype(bf16)
            added = dot(grad_scores, q[skip:], ((0,), (0,))) + dot(
                probs.astype(bf16), grad[skip:], ((0,), (0,))
            )
            added = added.astype(bf16).reshape(2, count, height, 2 * HD)
            where = (pl.ds(part * count, count), n ^ row)
            grad_near_ref[where] = added[0]
            grad_far_ref[where] = added[1]
            more = dot(grad_scores, keys)
            grad_q = lower(grad_q, lambda v: v + more, skip)
        return grad_q

    start = jnp.zeros((q.shape[0], 2 * HD), f32)
    grad_q = span(0, start) if spans == 1 else lax.fori_loop(0, spans, span, start)
    for n in range(chunks):
        grad_q_ref[pl.ds(pl.multiple_of((n ^ row) * height, 16), height), :] = grad_q[
            n * height : (n + 1) * height
        ]


def attention_specs(queries, kv, query_info, key_info):
    heads = queries.shape[1] // (2 * HD)
    rows = pl.BlockSpec((queries.shape[0], 2 * HD), lambda h: (0, h))
    keys = pl.BlockSpec(kv[0].shape[:3] + (2 * HD,), lambda h: (0, 0, 0, h))
    fixed = [
        pl.BlockSpec(memory_space=pltpu.SMEM),
        pl.BlockSpec(query_info.shape, lambda h: (0, 0)),
        pl.BlockSpec(key_info.shape, lambda h: (0, 0, 0)),
    ]
    bias = pltpu.VMEM((key_info.shape[0], queries.shape[0], key_info.shape[2]), f32)
    params = pltpu.CompilerParams(vmem_limit_bytes=56 * 2**20)
    return heads, rows, keys, fixed, bias, params


def work(kv, products):
    return pl.CostEstimate(
        flops=products * kv[0].size * 16000, bytes_accessed=8 * kv[0].size, transcendentals=0
    )


def attend(row, query_info, key_info, queries, kv):
    heads, rows, keys, fixed, bias, params = attention_specs(queries, kv, query_info, key_info)
    return pl.pallas_call(
        attend_kernel,
        grid=(heads,),
        in_specs=fixed + [rows, keys, keys],
        out_specs=rows,
        out_shape=jax.ShapeDtypeStruct(queries.shape, f32),
        scratch_shapes=[bias],
        compiler_params=params,
        cost_estimate=work(kv, 2),
    )(row, query_info, key_info, queries, *kv)


def attend_back(row, query_info, key_info, queries, kv, saved, grad):
    heads, rows, keys, fixed, bias, params = attention_specs(queries, kv, query_info, key_info)
    return pl.pallas_call(
        attend_back_kernel,
        grid=(heads,),
        in_specs=fixed + [rows, keys, keys, rows, rows],
        out_specs=[rows, keys, keys],
        out_shape=[jax.ShapeDtypeStruct(queries.shape, f32)]
        + [jax.ShapeDtypeStruct(t.shape, bf16) for t in kv],
        scratch_shapes=[bias],
        compiler_params=params,
        cost_estimate=work(kv, 5),
    )(row, query_info, key_info, queries, *kv, saved, grad)


def on_device(
    block_input,
    w_qkv,
    w_out,
    w_gate_up,
    w_down,
    norm_gains,
    cotangent,
    tok_seg,
    tok_pos,
    seg_parent,
):
    rows_n, b_n, x_n, c_n = (lax.axis_size(n) for n in ("za", "pb", "tx", "tc"))
    z, b, x, c = (lax.axis_index(n) for n in ("za", "pb", "tx", "tc"))
    shares = x_n * c_n
    plane = b_n * shares
    own, width = block_input.shape
    piece = width // plane

    def untangle(array, axis, index):
        count = array.shape[axis]
        for bit in range(count.bit_length() - 1):
            step = 1 << bit
            shape = array.shape[:axis] + (count // (2 * step), 2, step) + array.shape[axis + 1 :]
            flipped = jnp.flip(array.reshape(shape), axis + 1).reshape(array.shape)
            array = jnp.where((index >> bit) & 1 == 1, flipped, array)
        return array

    features = w_qkv.shape[2]
    heads = features // HD
    near = (heads + 1) // 2
    units = w_down.shape[0]
    near_units = min(units, (units // 2 + 127) // 128 * 128)
    w_kv = side_by_side(w_qkv[1], w_qkv[2])

    low = 32
    small = jnp.concatenate(
        [norm_gains.reshape(-1)] + [t.astype(bf16) for t in (tok_seg, tok_pos // low, tok_pos % low)]
    )
    small = jnp.pad(small, (0, width - small.shape[0]))[None]
    x_own = block_input
    x_parts = row_send(rows_of([x_own, small]))
    kv_full = plane_gather(*unbundle(turn(bundle([w_kv], [near * 2 * HD])), [2 * features], [near * 2 * HD]))
    q_full = plane_gather(*unbundle(turn(bundle([w_qkv[0]], [near * HD])), [features], [near * HD]))
    first = bundle([w_gate_up[0], w_out.T], [near_units, near * HD])
    second = bundle([w_gate_up[1], w_down.T], [near_units, near_units])
    x_parts, first, second = fence(x_parts, first, second)
    first = turn(first)
    small = rows_of([part[own:] for part in x_parts])
    small = [small] + [
        lax.ppermute(small, "pb", [(i, i ^ k) for i in range(b_n)]) for k in range(1, b_n)
    ]
    small = jnp.stack(small, axis=1)
    gains = small[..., : 2 * norm_gains.shape[1]].reshape(rows_n, b_n, 2, -1)
    group = tok_seg.shape[0]
    small = small[..., gains.shape[3] * 2 :][..., : 3 * group].astype(jnp.int32)
    seg_all = small[..., :group]
    pos_all = small[..., group : 2 * group] * low + small[..., 2 * group :]
    gains = untangle(untangle(gains, 0, z), 1, b).transpose(2, 0, 1, 3).reshape(2, width)
    gains = gains.astype(f32)

    pos_all = untangle(pos_all, 1, b).reshape(rows_n, b_n, x_n, c_n, own)
    seg_all = untangle(untangle(seg_all, 0, z), 1, b).reshape(pos_all.shape)
    index_all = jnp.arange(seg_all.size, dtype=jnp.int32).reshape(seg_all.shape)

    def for_group(array):
        array = lax.dynamic_slice_in_dim(array, b, 1, 1)
        array = lax.dynamic_slice_in_dim(array, x, 1, 2)
        return lax.dynamic_slice_in_dim(array, c, 1, 3).reshape(-1)

    def for_keys(array):
        array = untangle(array, 3, c).transpose(0, 3, 2, 1, 4).reshape(rows_n, 2, -1, 4, own)
        return array.transpose(0, 2, 1, 3, 4).reshape(-1, 8 * own)

    own_seg, own_index, pos_group = for_group(seg_all), for_group(index_all), for_group(pos_all)
    parent_seg, grand_seg = lineage(own_seg, seg_parent)
    query_info = jnp.stack([own_seg, parent_seg, grand_seg, own_index], axis=1)
    key_info = jnp.stack([for_keys(seg_all), for_keys(index_all)], axis=1)
    row = z.astype(jnp.int32).reshape(1)

    cosine, sine_table = rope_tables(pos_group)
    cot_own = cotangent.astype(f32)
    branch_f = (depth_scale * cot_own).astype(bf16)
    rows_a = rows_of([part[:own] for part in x_parts]).astype(f32)
    normed_a = ((rows_a * inverse_rms(rows_a)) * gains[0]).astype(bf16)
    group = rows_n * own
    mine = dot(normed_a, kv_full).reshape(group, heads, 2, HD)
    keys = rotate(mine[:, :, 0].reshape(group, -1), cosine, sine_table).astype(bf16)
    mine = side_by_side(keys, mine[:, :, 1].reshape(group, -1).astype(bf16))
    mine, second, branch_f, query_info, key_info = fence(
        mine, second, branch_f, query_info, key_info
    )
    gate_moved, out_moved = unbundle(after(first, mine), [units, features], [near_units, near * HD])
    out_full, gate_full = plane_gather(out_moved), plane_gather(gate_moved)
    second = turn(second)
    f_parts = row_send(branch_f)
    chips = b_n * x_n
    kv = exchange(jnp.broadcast_to(mine[None], (chips,) + mine.shape))
    queries = rotate(dot(after(normed_a, mine), q_full), cosine, sine_table)
    queries = side_by_side(queries.astype(bf16) * bf16(HD**-0.5), None)
    kv, second, queries, f_parts = fence(kv, second, queries, f_parts)
    up_moved, down_moved = unbundle(second, [units, units], [near_units, near_units])
    up_full = plane_gather(up_moved)
    kv = [t.reshape(chips, rows_n, own, -1) for t in (kv, swap_core(kv))]
    saved = attend(row, query_info, key_info, queries, kv)
    attended = saved.reshape(group, heads, 2, HD)[:, :, 1].reshape(group, -1).astype(bf16)
    mid_part = dot(attended, out_full, ((1,), (1,)))
    parts = row_split(mid_part)
    down_near = exchange(jnp.broadcast_to(down_moved[None], (chips,) + down_moved.shape))
    parts, down_near = fence(parts, down_near)
    down_near = down_near.reshape(-1, units)
    down_full = [down_near, swap_core(down_near)]
    mid = x_own.astype(f32) + depth_scale * row_sum(parts)
    inv_f = inverse_rms(mid)
    unit_f = mid * inv_f
    normed_f = rows_of(row_send((unit_f * gains[1]).astype(bf16)))
    grad_branch_f = rows_of(f_parts)
    gate = dot(normed_f, gate_full)
    up = dot(normed_f, up_full)
    sig = jax.nn.sigmoid(gate)
    silu = gate * sig
    hidden = (silu * up).astype(bf16)
    gf_twin = with_twin(grad_branch_f)
    nf_twin = with_twin(normed_f)
    grad_hidden = near_dot(columns(core_halves(grad_branch_f)), down_full)
    grad_gate = (grad_hidden * up * sig * (1.0 + gate * (1.0 - sig))).astype(bf16)
    grad_up = (grad_hidden * silu).astype(bf16)
    normed_part = dot(grad_gate, gate_full, ((1,), (1,))) + dot(grad_up, up_full, ((1,), (1,)))
    down_pair = pair_sum(gf_twin, hidden)
    normed_part, down_pair, hidden, grad_gate, grad_up, nf_twin = fence(
        normed_part, down_pair, hidden, grad_gate, grad_up, nf_twin
    )

    parts = row_split(normed_part)
    down_sum = exchange(down_pair)
    gate_pair = pair_sum(nf_twin, grad_gate)
    up_pair = pair_sum(nf_twin, grad_up)
    parts, down_sum, gate_pair, up_pair = fence(parts, down_sum, gate_pair, up_pair)
    grad_normed_f = row_sum(parts)
    gain_f = jnp.sum(grad_normed_f * unit_f, axis=0)
    grad_mid = cot_own + norm_back(grad_normed_f * gains[1], unit_f, inv_f)
    branch_a = (depth_scale * grad_mid).astype(bf16)

    parts = row_send(branch_a)
    gate_sum = exchange(gate_pair)
    down_sum = chip_sum(down_sum)
    output_part = columns([dot(after(hidden, branch_a), t, ((1,), (1,))) for t in down_full])
    na_twin = with_twin(after(normed_a, branch_a))
    attended = after(attended, branch_a)
    parts, gate_sum, down_sum, up_pair, output_part, na_twin, attended = fence(
        parts, gate_sum, down_sum, up_pair, output_part, na_twin, attended
    )
    two_back = bundle([down_sum, chip_sum(gate_sum)], [near_units, near_units])
    grad_branch_a = rows_of(parts)
    up_sum = exchange(up_pair)
    output_parts = row_split(output_part)
    grad_attended = dot(grad_branch_a, out_full).astype(bf16)
    grad_q, *grad_kv = attend_back(
        row, query_info, key_info, queries, kv, saved, side_by_side(None, grad_attended)
    )
    grad_q, grad_kv, up_sum, output_parts = fence(grad_q, grad_kv, up_sum, output_parts)

    grad_kv = (grad_kv[0].astype(f32) + swap_core(grad_kv[1]).astype(f32)).astype(bf16)
    grad_kv = grad_kv.reshape(chips, group, -1)
    grad_kv, grad_q, up_sum, two_back, grad_branch_a = fence(
        grad_kv, grad_q, up_sum, two_back, grad_branch_a
    )
    grad_kv = exchange(grad_kv)
    two_back = turn(two_back, True)
    up_back = bundle([chip_sum(up_sum)], [near_units])
    grad_q = grad_q.reshape(group, heads, 2, HD)[:, :, 0].reshape(group, -1) * HD**-0.5
    grad_q = rotate(grad_q, cosine, -sine_table).astype(bf16)
    q_pair = pair_sum(na_twin, grad_q)
    out_pair = pair_sum(with_twin(grad_branch_a), attended)
    two_pair = jnp.concatenate([q_pair, out_pair], axis=2)
    grad_kv, two_pair = fence(grad_kv, two_pair)
    two_sum = exchange(two_pair)
    grad_kv = jnp.sum(grad_kv.astype(f32), axis=0).reshape(group, heads, 2, HD)
    grad_k = rotate(grad_kv[:, :, 0].reshape(group, -1), cosine, -sine_table).astype(bf16)
    grad_kv = side_by_side(grad_k, grad_kv[:, :, 1].reshape(group, -1).astype(bf16))
    normed_part = dot(grad_q, q_full, ((1,), (1,))) + dot(grad_kv, kv_full, ((1,), (1,)))
    grad_kv, normed_part, two_back, up_back = fence(grad_kv, normed_part, two_back, up_back)
    parts = row_split(normed_part)
    kv_pair = pair_sum(na_twin, grad_kv)
    kv_pair, two_sum = fence(kv_pair, two_sum)
    kv_sum = exchange(kv_pair)
    two_sum = chip_sum(two_sum)
    parts, two_sum, up_back = fence(parts, two_sum, up_back)
    up_back = turn(up_back, True)
    grad_normed_a = row_sum(parts)
    output = mid + depth_scale * columns(core_halves(row_sum(output_parts)))
    kv_sum, up_back = fence(kv_sum, up_back)
    last_cuts = [near * 2 * HD, near * HD, near * HD]
    last_back = bundle([chip_sum(kv_sum), two_sum[:, :features], two_sum[:, features:]], last_cuts)
    last_back = turn(last_back, True)

    grad_w_down, grad_w_gate = unbundle(two_back, [units, units], [near_units, near_units])
    (grad_w_up,) = unbundle(up_back, [units], [near_units])
    grad_w_kv, grad_w_q, grad_w_out = unbundle(last_back, [2 * features, features, features], last_cuts)
    grad_gate_up = jnp.stack([grad_w_gate, grad_w_up]).astype(f32)
    grad_down = grad_w_down.astype(f32).T
    grad_out = grad_w_out.astype(f32).T
    grad_w_kv = grad_w_kv.reshape(piece, heads, 2, HD)
    grad_qkv = jnp.stack(
        [grad_w_q] + [grad_w_kv[:, :, n].reshape(piece, features) for n in range(2)]
    ).astype(f32)
    rows_own = x_own.astype(f32)
    inv_a = inverse_rms(rows_own)
    unit_a = rows_own * inv_a
    gain_a = jnp.sum(grad_normed_a * unit_a, axis=0)
    grad_input = grad_mid + norm_back(grad_normed_a * gains[0], unit_a, inv_a)
    gain_sum = jnp.stack([gain_a, gain_f])
    for axis, count in (("tc", c_n), ("tx", x_n), ("pb", b_n), ("za", rows_n)):
        for bit in range(count.bit_length() - 1):
            gain_sum = gain_sum + lax.ppermute(
                gain_sum, axis, [(i, i ^ (1 << bit)) for i in range(count)]
            )
    part = width // (rows_n * plane)
    place = ((z * b_n + b) * x_n + x) * c_n + c
    grad_gains = lax.dynamic_slice_in_dim(gain_sum, place * part, part, 1)
    return (output, grad_input, grad_qkv, grad_out, grad_gate_up, grad_down, grad_gains)


def solution(mesh):
    shares = mesh.shape["tensor"]
    devices = mesh.devices.reshape(shares, -1, shares // 2, 2)
    fine = Mesh(devices, ("za", "pb", "tx", "tc"))
    dp, tensor = ("za", "pb"), ("tx", "tc")
    in_specs = (
        P(dp + tensor, None),
        P(None, dp, tensor),
        P(tensor, dp),
        P(None, dp, tensor),
        P(tensor, dp),
        P(None, dp),
        P(dp + tensor, None),
        P(dp),
        P(dp),
        P(),
    )
    out_specs = (
        P(dp + tensor, None),
        P(dp + tensor, None),
        P(None, dp, tensor),
        P(tensor, dp),
        P(None, dp, tensor),
        P(tensor, dp),
        P(None, dp + tensor),
    )
    return jax.shard_map(
        on_device, mesh=fine, in_specs=in_specs, out_specs=out_specs, check_vma=False
    )
```
